768 devices in a mesh: dom: 96 (over z, x, core), grp: 8 (over y).
Axes of the slice: x: 4, y: 8, z: 12, core: 2. Of those that a mesh axis runs over, the one named last changes fastest.
Arguments:
- fields: float32 [6, 20, 393216], P(None, None, ('dom', 'grp')), may hold values from -6 to 6
- section_res: float32 [6, 20, 393216], P(None, None, ('dom', 'grp')), may hold values from -6 to 6
- derivative: float32 [3, 20, 20], replicated, may hold values from -1.25 to 1.25
- geometry: float32 [9, 393216], P(None, ('dom', 'grp')), may hold values from -6 to 6
- normals: float32 [3, 4, 393216], P(None, None, ('dom', 'grp')), may hold values from -6 to 6
- face_scale: float32 [4, 393216], P(None, ('dom', 'grp')), may hold values from 0.5 to 2
- lift_matrix: float32 [20, 40], replicated, may hold values from -1 to 1
- interp_q: float32 [23, 20], replicated, may hold values from -1.25 to 1.25
- project_q: float32 [20, 23], replicated, may hold values from -1.25 to 1.25
- mat_table: float32 [2, 6], replicated, may hold values from 0.2 to 1
- materials: int32 [393216], P(('dom', 'grp')), may hold values from 0 to 5
- profile: float32 [2, 23, 393216], P(None, None, ('dom', 'grp')), may hold values from 0.5 to 2
- face_partner: int32 [4, 393216], P(None, ('dom', 'grp')), may hold values from 0 to 2303, as said below
- send_faces: int32 [2, 98304], P(None, ('dom', 'grp')), may hold values from -1 to 2047, as said below
- spectra: float32 [32, 12, 24576], P(None, None, ('dom', 'grp')), may hold values from -6 to 6
- huy_slots: int32 [24576], P(('dom', 'grp')), may hold values from 0 to 2047, as said below
- huy_worker: int32 [24576, 1], P(('dom', 'grp')), may hold values from 0 to 7; in each aligned block of 32 rows (0 to 31, 32 to 63, ...) at most 8 rows name the same one
- huy_pos: float32 [3, 24576], P(None, ('dom', 'grp')), may hold values from -4 to 4
- wavenumber: float32 [32], replicated, may hold values from 1 to 6
- time_phase: float32 [32], replicated, may hold values from -3.140625 to 3.140625
Outputs:
- new_fields: float32 [6, 20, 393216], P(None, None, ('dom', 'grp'))
- new_res: float32 [6, 20, 393216], P(None, None, ('dom', 'grp'))
- new_spectra: float32 [32, 12, 24576], P(None, None, ('dom', 'grp'))
- worker_spectra: float32 [32, 12, 49152], P(None, None, ('dom', 'grp'))
- far_field: float32 [512, 128], P('grp')
The draws below stay inside these ranges and needn't reach their ends.
Inputs may be any that keep to these rules, and one draw needn't show every extreme that they name: `face_partner`: for slot s of a partition, the slot it meets in the coding of the exterior-trace step; slots below 2048 are paired both ways within the partition or meet themselves (the conducting skin); every live entry of a neighbour's list is met by exactly one slot. `send_faces`: each partition's 128 entries of a row list distinct slots, live ones first and -1 after; the upper list of partition p and the lower list of p + 1 have equal live counts, and some pair has all 128 live; partition 0 has no live lower entries and the last none upper. `huy_slots`: the 32 slots of a partition are distinct. `huy_worker`: among the 32 faces of one partition at most 8 name the same worker, and some partition names a worker exactly 8 times.
All inputs are finite; a program needn't handle non-finite values.
Results may differ from the reference program's by a relative error of at most 0.0003.
Values sent between devices are 32-bit elements; how exact they have to be, the bound alone decides.
No kernel may reach another device: no remote copies, remote signals or barrier semaphores. Data moves between devices by JAX's collectives and lax.ppermute only.
A program may use at most 64 MiB of HBM per device.

```python
import math
import jax
import jax.numpy as jnp
import numpy as np
from jax import lax

E_DEV = 512
SHARED = 128
HDEV = 32
CAP = 8
FREQS = 32
DIRS = 512
NP = 20
NFP = 10
QPTS = 23
MATS = 6
E_TOTAL = 393216
HUYGENS = 24576
WORKER_SLOTS = 49152
N_GRP = 8


def shared_lists(key):
    devices = E_TOTAL // E_DEV
    slot_count = 4 * E_DEV
    key_bounds = jax.random.fold_in(key, 11)
    key_orders = jax.random.fold_in(key, 12)
    bounds = jax.random.randint(key_bounds, (devices,), SHARED // 2, SHARED + 1).astype(jnp.int32)
    chosen = jax.random.randint(jax.random.fold_in(key_bounds, 1), (), 0, devices - 1)
    bounds = bounds.at[chosen].set(SHARED)
    bounds = bounds.at[devices - 1].set(0)
    below = jnp.concatenate([jnp.zeros((1,), jnp.int32), bounds[:-1]])
    orders = jax.vmap(lambda sub_key: jax.random.permutation(sub_key, slot_count))(jax.random.split(key_orders, devices)).astype(jnp.int32)
    return (below, bounds, orders)


def draw_face_partner(key, part):
    below, above, orders = shared_lists(key)
    slot_count = 4 * E_DEV
    spare = slot_count - 2 * SHARED
    pairs = spare * 9 // 20

    def one_device(order, count_below, count_above):
        position = jnp.arange(slot_count, dtype=jnp.int32)
        offset = position - 2 * SHARED
        mate = order[jnp.clip(2 * SHARED + jnp.bitwise_xor(offset, 1), 0, slot_count - 1)]
        remote_low = jnp.where(position < count_below, slot_count + position, order)
        remote_high = jnp.where(position - SHARED < count_above, slot_count + position, order)
        local_side = jnp.where(offset < 2 * pairs, mate, order)
        chosen_value = jnp.where(position < SHARED, remote_low, jnp.where(position < 2 * SHARED, remote_high, local_side))
        return jnp.zeros((slot_count,), jnp.int32).at[order].set(chosen_value.astype(jnp.int32))
    mapped = jax.vmap(one_device)(orders, below, above)
    return mapped.reshape(-1, 4, E_DEV).transpose(1, 0, 2).reshape(4, -1)


def draw_send_faces(key, part):
    below, above, orders = shared_lists(key)
    column = jnp.arange(SHARED, dtype=jnp.int32)
    low_row = jnp.where(column[None, :] < below[:, None], orders[:, :SHARED], -1)
    high_row = jnp.where(column[None, :] < above[:, None], orders[:, SHARED:2 * SHARED], -1)
    return jnp.stack([low_row, high_row]).reshape(2, -1).astype(jnp.int32)


def draw_huy_slots(key, part):
    key = jax.random.fold_in(key, 5)
    devices = E_TOTAL // E_DEV
    picked = jax.vmap(lambda sub_key: jax.random.permutation(sub_key, 4 * E_DEV)[:HDEV])(jax.random.split(key, devices))
    return picked.reshape(-1).astype(jnp.int32)


def with_ends(entries, stream_key, low, top_value):
    shape = entries.shape
    place = [jax.random.randint(jax.random.fold_in(stream_key, axis), (), 0, shape[axis]) for axis in range(len(shape))]
    entries = entries.at[tuple(place)].set(low)
    longest = shape.index(max(shape))
    place[longest] = (place[longest] + 1) % shape[longest]
    return entries.at[tuple(place)].set(top_value)


def level_of(stream_key, dims, cuts, smallest, high):
    def one(dim, shards_of):
        heights = jax.random.uniform(jax.random.fold_in(jax.random.fold_in(stream_key, 6), dim), (shards_of,), jnp.float32, smallest / len(cuts), high / len(cuts))
        return jnp.repeat(jnp.exp(heights), dims[dim] // shards_of).reshape((-1,) + (1,) * (len(dims) - dim - 1))

    gain = one(*cuts[0])
    for cut in cuts[1:]:
        gain = gain * one(*cut)
    return gain


def routed_block(rng, own, number, rows, count, top, bound, slope):
    ranking = jax.random.permutation(rng, count)
    packed, ordinary = shares(count, rows * top, bound, slope, True), shares(count, rows * top, bound, slope, False)
    places = jnp.arange(count)

    def named(tallies, offset_by):
        used = int((tallies > 0).sum())
        fixed = max(1, used // 4)
        shifted = fixed + (places - fixed + offset_by * (used - fixed)) % max(1, count - fixed)
        return jnp.zeros((count,), jnp.int32).at[ranking[jnp.where(places < fixed, places, shifted)]].set(jnp.asarray(tallies, jnp.int32))

    tallies = jnp.where(number % 4 == 0, named(packed, number // 4), named(ordinary, number - number // 4 - 1))
    mixed = jax.random.permutation(jax.random.fold_in(own, 3), count)
    donor, receiver = mixed[0:count // 2 * 2:2], mixed[1:count // 2 * 2:2]
    slack = jnp.minimum(tallies[donor] - 1, bound - tallies[receiver]) // 2
    slack = jnp.where((donor == ranking[0]) | (receiver == ranking[0]) | (tallies[receiver] == 0), 0, jnp.maximum(slack, 0))
    shifted = jax.random.randint(jax.random.fold_in(own, 4), (count // 2,), 0, 1 << 20) % (slack + 1)
    tallies = tallies.at[donor].add(-shifted).at[receiver].add(shifted)
    items = jnp.searchsorted(jnp.cumsum(tallies), jnp.arange(rows * top), side="right").astype(jnp.int32)
    table = items.reshape(top, rows).T
    table = table[jax.random.permutation(jax.random.fold_in(own, 1), rows)]
    offset_by = jax.random.randint(jax.random.fold_in(own, 2), (rows, 1), 0, top)
    return jnp.take_along_axis(table, (jnp.arange(top)[None, :] + offset_by) % top, axis=1)


def shares(number_of, total, bound, slope, full):
    portions = [(1 << 20) // math.isqrt(standing ** slope) + 1 for standing in range(1, number_of + 1)]
    largest = bound if full else min(bound, max(-(-total // number_of), total * portions[0] // sum(portions)))
    least = 1 if total - largest >= number_of - 1 else 0
    given, rest = [largest] + [least] * (number_of - 1), total - largest - least * (number_of - 1)
    while rest > 0:
        candidates = [i for i in range(1, number_of) if given[i] < largest] or [i for i in range(1, number_of) if given[i] < bound]
        pool, remaining = sum([portions[i] for i in candidates]), rest
        for i in candidates:
            extra = min(bound - given[i], max(1, remaining * portions[i] // pool), rest)
            given[i] = given[i] + extra
            rest = rest - extra
    return np.array(given)


def normal_values(rng, shape, width, bound, cuts=(), held_as=jnp.bfloat16):
    gain = level_of(rng, shape, cuts, -0.22, 0.18) if cuts else 1.0
    drawn = jax.random.normal(rng, shape, jnp.float32) * width * gain
    return jnp.minimum(jnp.maximum(drawn, -bound), bound).astype(held_as)


def setup_inputs(seed: int = 0) -> dict:
    arg_keys = jax.random.split(jax.random.key(seed), 21)
    fields = normal_values(arg_keys[0], (6, NP, E_TOTAL), 1.0, 6.0, ((2, 768),), jnp.float32)
    section_res = normal_values(arg_keys[1], (6, NP, E_TOTAL), 1.0, 6.0, ((2, 768),), jnp.float32)
    derivative = normal_values(arg_keys[2], (3, NP, NP), NP ** -0.5, 1.25, (), jnp.float32)
    geometry = normal_values(arg_keys[3], (9, E_TOTAL), 1.0, 6.0, ((1, 768),), jnp.float32)
    normals = normal_values(arg_keys[4], (3, 4, E_TOTAL), 1.0, 6.0, ((2, 768),), jnp.float32)
    face_scale = jnp.clip(jnp.exp(math.log(2.0) - 1.3862944 * jax.random.uniform(arg_keys[5], (4, E_TOTAL), jnp.float32) ** level_of(arg_keys[5], (4, E_TOTAL), ((1, 768),), -0.2, 0.2)), 0.5, 2.0)
    lift_matrix = normal_values(arg_keys[6], (NP, 4 * NFP), (4 * NFP) ** -0.5, 1.0, (), jnp.float32)
    interp_q = normal_values(arg_keys[7], (QPTS, NP), NP ** -0.5, 1.25, (), jnp.float32)
    project_q = normal_values(arg_keys[8], (NP, QPTS), QPTS ** -0.5, 1.25, (), jnp.float32)
    mat_table = jnp.clip(jnp.exp(jax.random.uniform(arg_keys[9], (2, MATS), jnp.float32, math.log(0.2), math.log(1.0))), 0.2, 1.0)
    materials = with_ends(jax.random.randint(arg_keys[10], (E_TOTAL,), 0, MATS), jax.random.fold_in(arg_keys[10], 1), 0, MATS - 1).astype(jnp.int32)
    profile = jnp.clip(jnp.exp(math.log(2.0) - 1.3862944 * jax.random.uniform(arg_keys[11], (2, QPTS, E_TOTAL), jnp.float32) ** level_of(arg_keys[11], (2, QPTS, E_TOTAL), ((2, 768),), -0.2, 0.2)), 0.5, 2.0)
    face_partner = draw_face_partner(jax.random.fold_in(arg_keys[20], 71), 0)
    send_faces = draw_send_faces(jax.random.fold_in(arg_keys[20], 71), 0)
    spectra = normal_values(arg_keys[14], (FREQS, 12, HUYGENS), 1.0, 6.0, ((2, 768),), jnp.float32)
    huy_slots = draw_huy_slots(jax.random.fold_in(arg_keys[20], 71), 0)
    huy_worker_keys = jax.random.split(jax.random.fold_in(arg_keys[16], 1), HUYGENS // HDEV)
    huy_worker_turns = jax.random.permutation(jax.random.fold_in(arg_keys[16], 3), HUYGENS // HDEV)
    huy_worker = jax.vmap(lambda own, number: routed_block(jax.random.fold_in(arg_keys[16], 2), own, number, HDEV, N_GRP, 1, CAP, 1))(huy_worker_keys, huy_worker_turns).reshape((HUYGENS, 1))
    huy_pos = jnp.clip(jax.random.uniform(arg_keys[17], (3, HUYGENS), jnp.float32, -4.0, 4.0) * level_of(arg_keys[17], (3, HUYGENS), ((1, 768),), -0.4, 0.0), -4.0, 4.0)
    wavenumber = jnp.clip(jnp.exp(jax.random.uniform(arg_keys[18], (FREQS,), jnp.float32, math.log(1.0), math.log(6.0))), 1.0, 6.0)
    time_phase = jnp.clip(jax.random.uniform(arg_keys[19], (FREQS,), jnp.float32, -3.140625, 3.140625), -3.140625, 3.140625)
    return dict(fields=fields, section_res=section_res, derivative=derivative, geometry=geometry, normals=normals, face_scale=face_scale, lift_matrix=lift_matrix, interp_q=interp_q, project_q=project_q, mat_table=mat_table, materials=materials, profile=profile, face_partner=face_partner, send_faces=send_faces, spectra=spectra, huy_slots=huy_slots, huy_worker=huy_worker, huy_pos=huy_pos, wavenumber=wavenumber, time_phase=time_phase)


rk_alpha = -0.4178904745
rk_beta = 0.3792103129
time_step = 0.5
freq_block = 8
highest = lax.Precision.HIGHEST

def face_nodes():
    lattice = [(along_a, along_b, along_c) for along_c in range(4) for along_b in range(4 - along_c) for along_a in range(4 - along_b - along_c)]
    checkers = [lambda point_abc: point_abc[2] == 0, lambda point_abc: point_abc[1] == 0, lambda point_abc: sum(point_abc) == 3, lambda point_abc: point_abc[0] == 0]
    face_rows = []
    for checker in checkers:
        face_rows.append([node_id for node_id, point_abc in enumerate(lattice) if checker(point_abc)])
    return np.array(face_rows, dtype=np.int32)

def face_traces(values):
    node_table = face_nodes()
    elements = values.shape[2]
    picked = values[:, node_table.reshape(-1), :]
    picked = picked.reshape(values.shape[0], 4, node_table.shape[1], elements)
    return picked.transpose(0, 2, 1, 3).reshape(values.shape[0], node_table.shape[1], 4 * elements)

def cross_product(first_vec, second_vec):
    return jnp.stack([first_vec[1] * second_vec[2] - first_vec[2] * second_vec[1], first_vec[2] * second_vec[0] - first_vec[0] * second_vec[2], first_vec[0] * second_vec[1] - first_vec[1] * second_vec[0]])

def section_update(fields, section_res, derivative, geometry, normals, face_scale, lift_matrix, interp_q, project_q, mat_table, materials, profile, partner, from_below, from_above):
    elements = fields.shape[2]
    slot_count = 4 * elements
    face_nodes_count = lift_matrix.shape[1] // 4
    derivs = jnp.einsum('rij,cje->rcie', derivative, fields, precision=highest)
    metric = geometry.reshape(3, 3, elements)

    def spatial(direction):
        return metric[0, direction] * derivs[0] + metric[1, direction] * derivs[1] + metric[2, direction] * derivs[2]
    along_x, along_y, along_z = (spatial(0), spatial(1), spatial(2))
    curl_h = jnp.stack([along_y[5] - along_z[4], along_z[3] - along_x[5], along_x[4] - along_y[3]])
    curl_e = jnp.stack([along_y[2] - along_z[1], along_z[0] - along_x[2], along_x[1] - along_y[0]])
    inside = face_traces(fields)
    extended = jnp.concatenate([inside, from_below, from_above], axis=2)
    outside = jnp.take(extended, partner, axis=2)
    on_skin = (partner == jnp.arange(slot_count, dtype=jnp.int32))[None, None, :]
    jump_e = jnp.where(on_skin, -inside[:3], outside[:3]) - inside[:3]
    jump_h = outside[3:] - inside[3:]
    normal = normals.reshape(3, slot_count)[:, None, :]
    normal_e = lax.optimization_barrier(jnp.sum(normal * jump_e, axis=0))
    normal_h = lax.optimization_barrier(jnp.sum(normal * jump_h, axis=0))
    half_scale = 0.5 * face_scale.reshape(slot_count)
    flux_e = (cross_product(normal, jump_h) + jump_e - normal_e * normal) * half_scale
    flux_h = (-cross_product(normal, jump_e) + jump_h - normal_h * normal) * half_scale
    flux_all = jnp.concatenate([flux_e, flux_h]).reshape(6, face_nodes_count, 4, elements)
    flux_all = flux_all.transpose(0, 2, 1, 3).reshape(6, 4 * face_nodes_count, elements)
    lifted = jnp.einsum('ik,cke->cie', lift_matrix, flux_all, precision=highest)
    raw_rate = jnp.concatenate([curl_h, -curl_e]) + lifted
    onehot = (materials[None, :] == jnp.arange(mat_table.shape[1], dtype=jnp.int32)[:, None]).astype(jnp.float32)
    base_coef = jnp.dot(mat_table, onehot, precision=highest)
    weights = base_coef[:, None, :] * profile
    at_points = jnp.einsum('qj,cje->cqe', interp_q, raw_rate, precision=highest)
    at_points = at_points.reshape(2, 3, interp_q.shape[0], elements) * weights[:, None]
    adjusted = jnp.einsum('jq,cqe->cje', project_q, at_points.reshape(6, interp_q.shape[0], elements), precision=highest)
    new_res = rk_alpha * section_res + time_step * adjusted
    new_fields = fields + rk_beta * new_res
    return (new_fields, new_res)

def huygens_currents(new_fields, normals, huy_slots):
    averaged = lax.optimization_barrier(jnp.mean(face_traces(new_fields), axis=1))
    picked = jnp.take(averaged, huy_slots, axis=1)
    normal = jnp.take(normals.reshape(3, -1), huy_slots, axis=1)
    return jnp.concatenate([cross_product(normal, picked[3:]), -cross_product(normal, picked[:3])])

def add_spectra(spectra, current, time_phase):
    real_part = jnp.cos(time_phase)[:, None, None] * current[None]
    imag_part = jnp.sin(time_phase)[:, None, None] * current[None]
    return spectra + jnp.concatenate([real_part, imag_part], axis=1)

def far_terms(rows_spec, rows_pos, wavenumber, first_row, row_count, norm_scale):
    row_ids = first_row + jnp.arange(row_count, dtype=jnp.int32)
    height = 1.0 - (2.0 * row_ids.astype(jnp.float32) + 1.0) / DIRS
    radius = jnp.sqrt(1.0 - height * height)
    azimuth = (row_ids * 381966 % 1000000).astype(jnp.float32) * 1e-06 * (2.0 * math.pi)
    cos_turn = jnp.cos(azimuth)
    sin_turn = jnp.sin(azimuth)
    heading = jnp.stack([radius * cos_turn, radius * sin_turn, height])
    theta_hat = jnp.stack([height * cos_turn, height * sin_turn, -radius])
    phi_hat = jnp.stack([-sin_turn, cos_turn, jnp.zeros_like(cos_turn)])
    path_length = jnp.einsum('xr,xd->rd', rows_pos, heading, precision=highest)
    freq_count = rows_spec.shape[0]
    blocks_spec = rows_spec.reshape(freq_count // freq_block, freq_block, 12, rows_spec.shape[2])
    blocks_wave = wavenumber.reshape(freq_count // freq_block, freq_block)

    def project(summed_vec, unit_vec):
        return unit_vec[0] * summed_vec[:, 0] + unit_vec[1] * summed_vec[:, 1] + unit_vec[2] * summed_vec[:, 2]

    def components(summed):
        electric = summed[:, :3]
        magnetic = summed[:, 3:]
        return (project(electric, theta_hat) + project(magnetic, phi_hat), project(magnetic, theta_hat) - project(electric, phi_hat))

    def one_block(block_pair):
        spec_block, wave_block = block_pair
        phase_angle = wave_block[:, None, None] * path_length[None]
        with_cos = jnp.einsum('fcr,frd->fcd', spec_block, jnp.cos(phase_angle), precision=highest)
        with_sin = jnp.einsum('fcr,frd->fcd', spec_block, jnp.sin(phase_angle), precision=highest)
        real_sum = with_cos[:, :6] - with_sin[:, 6:]
        imag_sum = with_sin[:, :6] + with_cos[:, 6:]
        theta_re, phi_re = components(real_sum)
        theta_im, phi_im = components(imag_sum)
        return jnp.stack([theta_re, theta_im, phi_re, phi_im], axis=1)
    result = lax.map(one_block, (blocks_spec, blocks_wave))
    result = result.reshape(freq_count, 4, row_count).transpose(1, 0, 2).reshape(4 * freq_count, row_count)
    return result.T * norm_scale

def reference(fields, section_res, derivative, geometry, normals, face_scale, lift_matrix, interp_q, project_q, mat_table, materials, profile, face_partner, send_faces, spectra, huy_slots, huy_worker, huy_pos, wavenumber, time_phase):
    devices = E_TOTAL // E_DEV

    def split_last(stacked):
        leading = stacked.shape[:-1]
        return jnp.moveaxis(stacked.reshape(leading + (devices, stacked.shape[-1] // devices)), -2, 0)

    def join_last(stacked):
        moved = jnp.moveaxis(stacked, 0, -2)
        return moved.reshape(moved.shape[:-2] + (-1,))
    dev_fields = split_last(fields)
    dev_res = split_last(section_res)
    dev_geometry = split_last(geometry)
    dev_normals = split_last(normals)
    dev_scale = split_last(face_scale)
    dev_materials = split_last(materials)
    dev_profile = split_last(profile)
    dev_partner = split_last(face_partner)
    dev_send = split_last(send_faces)
    dev_slots = split_last(huy_slots)
    dev_spec = split_last(spectra)
    dev_pos = split_last(huy_pos)

    def send_rows(device_items):
        values, send_lists = device_items
        inside = face_traces(values)
        is_live = send_lists >= 0
        picked = jnp.take(inside, jnp.where(is_live, send_lists, 0).reshape(-1), axis=2)
        picked = picked.reshape(6, inside.shape[1], 2, send_lists.shape[1]).transpose(2, 0, 1, 3)
        return picked * is_live[:, None, None, :].astype(jnp.float32)
    sent = lax.map(send_rows, (dev_fields, dev_send))
    zero_row = jnp.zeros_like(sent[:1, 0])
    lowers = jnp.concatenate([zero_row, sent[:-1, 1]], axis=0)
    uppers = jnp.concatenate([sent[1:, 0], zero_row], axis=0)

    def per_device(device_items):
        values, residue, metric, normal, scale_face, material_ids, coat_profile, partner, from_below, from_above, slot_ids, spec_rows = device_items
        out_fields, out_res = section_update(values, residue, derivative, metric, normal, scale_face, lift_matrix, interp_q, project_q, mat_table, material_ids, coat_profile, partner.reshape(-1), from_below, from_above)
        current = huygens_currents(out_fields, normal, slot_ids)
        return (out_fields, out_res, add_spectra(spec_rows, current, time_phase))
    out_fields, out_res, out_spec = lax.map(per_device, (dev_fields, dev_res, dev_geometry, dev_normals, dev_scale, dev_materials, dev_profile, dev_partner, lowers, uppers, dev_slots, dev_spec))
    new_fields = join_last(out_fields)
    new_res = join_last(out_res)
    new_spectra = join_last(out_spec)
    workers = huy_worker[:, 0].reshape(devices, HDEV)
    onehot = (workers[:, :, None] == jnp.arange(N_GRP, dtype=jnp.int32)[None, None, :]).astype(jnp.int32)
    slot_rank = lax.optimization_barrier(jnp.sum(jnp.cumsum(onehot, axis=1) * onehot, axis=2)) - 1
    device_ids = jnp.arange(devices, dtype=jnp.int32)[:, None]
    target = ((device_ids // N_GRP * N_GRP + workers) * N_GRP + device_ids % N_GRP) * CAP + slot_rank
    worker_spectra = jnp.zeros((FREQS, 12, WORKER_SLOTS), jnp.float32).at[:, :, target.reshape(-1)].set(new_spectra)
    norm_scale = 1.0 / math.sqrt(HUYGENS)

    def accumulate(running, device_items):
        spec_rows, pos_rows = device_items
        return (running + far_terms(spec_rows, pos_rows, wavenumber, 0, DIRS, norm_scale), None)
    far_field, _ = lax.scan(accumulate, jnp.zeros((DIRS, 4 * FREQS), jnp.float32), (out_spec, dev_pos))
    return (new_fields, new_res, new_spectra, worker_spectra, far_field)
```

```python
import math

import jax
import jax.numpy as jnp
import numpy as np
from jax import lax
from jax.experimental import pallas as pl
from jax.experimental.pallas import tpu as pltpu
from jax.sharding import Mesh
from jax.sharding import PartitionSpec as P

CAP = 8
DIRS = 512
FREQS = 32
ELEMS = 512
HDEV = 32
SHARED = 128
NP = 20
NFP = 10
QPTS = 23
MATS = 6
GRP = 8
GROUPS = 4
CHUNK = 8
MEMBERS = 64
ROWS = CHUNK + 3

rk_alpha = -0.4178904745
rk_beta = 0.3792103129
time_step = 0.5
highest = lax.Precision.HIGHEST
f32 = jnp.float32
bf16 = jnp.bfloat16

COS_POLY = (
    0.9999999891722178,
    -19.73920453207716,
    64.9391189830781,
    -85.4501655363007,
    60.167831622719845,
    -25.968312914489402,
    6.5296098973910475,
)
SIN_POLY = (
    6.283185302554009,
    -41.341700417566,
    81.6051319576367,
    -76.7030251163624,
    42.026002315250366,
    -14.900114558517526,
    3.2384947548003575,
)
ROUNDER = 12582912.0


def face_nodes():
    lattice = [
        (along_a, along_b, along_c)
        for along_c in range(4)
        for along_b in range(4 - along_c)
        for along_a in range(4 - along_b - along_c)
    ]
    checkers = [
        lambda point_abc: point_abc[2] == 0,
        lambda point_abc: point_abc[1] == 0,
        lambda point_abc: sum(point_abc) == 3,
        lambda point_abc: point_abc[0] == 0,
    ]
    return np.array(
        [[n for n, abc in enumerate(lattice) if checker(abc)] for checker in checkers],
        dtype=np.int32,
    )


def constants(dir_order, norm_scale):
    nodes = face_nodes()
    select = np.zeros((64, NP), np.float32)
    on_face = np.zeros((32, 4), np.float32)
    widen = np.zeros((4 * NFP, 192), np.float32)
    for face in range(4):
        for j in range(NFP):
            select[face * 16 + j, nodes[face, j]] = 1.0
            on_face[nodes[face, j], face] = 1.0
            for copy in range(3):
                widen[face * NFP + j, copy * 64 + face * 16 + j] = 1.0
    widen_q = np.zeros((QPTS, 96), np.float32)
    for q in range(QPTS):
        for copy in range(3):
            widen_q[q, copy * 32 + q] = 1.0
    spread = np.zeros((HDEV, 8 * HDEV), np.float32)
    for h in range(HDEV):
        spread[h, h::HDEV] = 1.0
    row_ids = dir_order.astype(np.int64)
    height = 1.0 - (2.0 * row_ids + 1.0) / DIRS
    radius = np.sqrt(1.0 - height * height)
    azimuth = (row_ids * 381966 % 1000000) * 1e-06 * (2.0 * math.pi)
    cos_turn, sin_turn = np.cos(azimuth), np.sin(azimuth)
    zero = np.zeros_like(height)
    directions = np.stack(
        [radius * cos_turn, radius * sin_turn, height]
        + [norm_scale * v for v in (height * cos_turn, height * sin_turn, -radius)]
        + [norm_scale * v for v in (-sin_turn, cos_turn)]
        + [zero] * 8
    ).astype(np.float32)
    return select, on_face, widen, widen_q, spread, directions


def high_low(values):
    high = values.astype(bf16)
    return high, (values - high.astype(f32)).astype(bf16)


def mm(a, b):
    return jnp.dot(a, b, preferred_element_type=f32)


def mm_exact(a, b):
    return jnp.dot(a, b, preferred_element_type=f32, precision=highest)


def one_hot_rows(count, base, row):
    step = min(count, 256)
    ids = lax.broadcasted_iota(jnp.int32, (step, row.shape[1]), 0).astype(f32).astype(bf16)
    pieces = []
    for start in range(base, base + count, step):
        local = row - start
        local = jnp.where((local >= 0) & (local < step), local, -1).astype(f32).astype(bf16)
        pieces.append(jnp.where(ids == local, jnp.ones((), bf16), jnp.zeros((), bf16)))
    return pieces[0] if len(pieces) == 1 else jnp.concatenate(pieces, axis=0)


def cos_sin_turns(turns):
    part = turns - ((turns + ROUNDER) - ROUNDER)
    square = part * part
    cos_part = COS_POLY[-1] * square + COS_POLY[-2]
    sin_part = SIN_POLY[-1] * square + SIN_POLY[-2]
    for c, s in zip(COS_POLY[-3::-1], SIN_POLY[-3::-1]):
        cos_part = cos_part * square + c
        sin_part = sin_part * square + s
    return cos_part, sin_part * part


def column_of(row):
    n = row.shape[1]
    eye = lax.broadcasted_iota(jnp.int32, (n, n), 0) == lax.broadcasted_iota(jnp.int32, (n, n), 1)
    return jnp.sum(jnp.where(eye, row, 0.0), axis=1, keepdims=True)


class Fetched:
    def __init__(self, source, target, sem):
        self.copy = pltpu.make_async_copy(source, target, sem)
        self.target = target
        self.waited = False
        self.copy.start()

    def ref(self):
        if not self.waited:
            self.copy.wait()
            self.waited = True
        return self.target

    def __getitem__(self, key):
        return self.ref()[key]


class Sent:
    def __init__(self, source, target, sem):
        self.source, self.target, self.sem = source, target, sem
        self.copies = []

    def __getitem__(self, key):
        return self.source[key]

    def __setitem__(self, key, value):
        self.source[key] = value

    @property
    def shape(self):
        return self.source.shape

    def send(self, *index):
        source, target = self.source, self.target
        if index:
            source, target = source.at[index], target.at[index]
        sem = self.sem.at[len(self.copies)]
        self.copies.append(pltpu.make_async_copy(source, target, sem))
        self.copies[-1].start()


def moving(kernel, first, fetched, n_in, sent, n_out):
    def wrapped(*refs):
        ins, outs, rest = refs[:n_in], refs[n_in : n_in + n_out], refs[n_in + n_out :]
        targets, sems, rest = rest[:fetched], rest[fetched], rest[fetched + 1 :]
        held = [Fetched(ins[first + i], targets[i], sems.at[i]) for i in range(fetched)]
        going = []
        if sent:
            sources, sems, rest = rest[:sent], rest[sent], rest[sent + 1 :]
            going = [Sent(sources[i], outs[i], sems.at[i]) for i in range(sent)]
        kernel(*ins[:first], *held, *ins[first + fetched :], *going, *outs[sent:], *rest)
        for one in held:
            one.ref()
        for one in going:
            for copy in one.copies:
                copy.wait()

    return wrapped


def call(kernel, name, operands, first, fetched, outs, sent, scratch, limit, micros):
    moved = operands[first : first + fetched]
    scratch_shapes = [pltpu.VMEM(a.shape, a.dtype) for a in moved]
    scratch_shapes.append(pltpu.SemaphoreType.DMA((fetched,)))
    if sent:
        scratch_shapes += [pltpu.VMEM(o.shape, o.dtype) for o in outs[:sent]]
        scratch_shapes.append(pltpu.SemaphoreType.DMA((sent, GROUPS)))
    return pl.pallas_call(
        moving(kernel, first, fetched, len(operands), sent, len(outs)),
        out_shape=tuple(outs),
        in_specs=[SMEM] * first + [HBM] * fetched + [VMEM] * (len(operands) - first - fetched),
        out_specs=tuple([HBM] * sent + [VMEM] * (len(outs) - sent)),
        scratch_shapes=scratch_shapes + scratch,
        cost_estimate=pl.CostEstimate(flops=int(micros * 1e8), bytes_accessed=4 << 20, transcendentals=0),
        compiler_params=pltpu.CompilerParams(vmem_limit_bytes=limit),
        name=name,
    )(*operands)


def trace_kernel(fields_ref, send_ref, select_ref, trace_ref, lower_ref, upper_ref):
    select = select_ref[...].astype(bf16)
    for c in range(6):
        for part, half in enumerate(high_low(fields_ref[c])):
            picked = mm(select, half).astype(bf16)
            for face in range(4):
                trace_ref[part * 96 + c * 16 : part * 96 + (c + 1) * 16, face * ELEMS : (face + 1) * ELEMS] = picked[
                    face * 16 : (face + 1) * 16
                ]
    trace_ref.send()
    send = send_ref[...]
    total = [jnp.zeros((192, SHARED), f32), jnp.zeros((192, SHARED), f32)]
    for face in range(4):
        held = trace_ref[:, face * ELEMS : (face + 1) * ELEMS]
        for row in range(2):
            total[row] = total[row] + mm(held, one_hot_rows(ELEMS, face * ELEMS, send[row : row + 1]))
    lower_ref[...] = total[0][:96] + total[0][96:]
    upper_ref[...] = total[1][:96] + total[1][96:]


def early_kernel(
    wave_ref,
    table_ref,
    fields_ref,
    partner_ref,
    derivative_ref,
    geometry_ref,
    normals_ref,
    interp_ref,
    project_ref,
    lift_ref,
    materials_ref,
    profile_ref,
    slots_ref,
    pos_ref,
    widen_ref,
    widen_q_ref,
    dirs_ref,
    trace_ref,
    phase_ref,
    jump_ref,
    curl_ref,
    weight_ref,
    lift_out_ref,
    project_out_ref,
    normal_out_ref,
    pad_ref,
    grad_ref,
):
    heading = dirs_ref[...]
    pos = pos_ref[...]
    path = jnp.zeros((HDEV, DIRS), f32)
    for k in range(3):
        path = path + column_of(pos[k : k + 1]) * heading[k : k + 1]
    for f in range(FREQS):
        cos_part, sin_part = cos_sin_turns(path * (wave_ref[f] * (0.5 / math.pi)))
        rows = slice((f % 8) * HDEV, (f % 8 + 1) * HDEV)
        for place, half in enumerate(high_low(cos_part) + high_low(sin_part)):
            phase_ref[f // 8, place, rows, :] = half
        if f % 8 == 7:
            phase_ref.send(f // 8)

    slots = slots_ref[...]
    pick = one_hot_rows(ELEMS, 0, slots & (ELEMS - 1))
    face_id = lax.shift_right_logical(slots, 9)
    match = lax.broadcasted_iota(jnp.int32, (4, HDEV), 0) == face_id
    normal_out_ref[...] = jnp.zeros((8, HDEV), f32)
    for k in range(3):
        high, low = high_low(normals_ref[k])
        normal_out_ref[k : k + 1, :] = jnp.sum(
            jnp.where(match, mm(high, pick) + mm(low, pick), 0.0), axis=0, keepdims=True
        )
    normal_out_ref.send()

    interp = interp_ref[...]
    pad_ref[...] = jnp.zeros((96, NP), f32)
    for r in range(3):
        pad_ref[r * 32 : r * 32 + QPTS, :] = mm_exact(interp, derivative_ref[r])
    slope_high, slope_low = high_low(pad_ref[...])
    for c in range(6):
        high, low = high_low(fields_ref[c])
        grad_ref[c] = mm(slope_high, high) + (mm(slope_low, high) + mm(slope_high, low))

    def along(k, c):
        return (
            geometry_ref[k : k + 1, :] * grad_ref[c, 0:32, :]
            + geometry_ref[3 + k : 4 + k, :] * grad_ref[c, 32:64, :]
            + geometry_ref[6 + k : 7 + k, :] * grad_ref[c, 64:96, :]
        )

    curl_ref[0] = along(1, 5) - along(2, 4)
    curl_ref[1] = along(2, 3) - along(0, 5)
    curl_ref[2] = along(0, 4) - along(1, 3)
    curl_ref[3] = along(2, 1) - along(1, 2)
    curl_ref[4] = along(0, 2) - along(2, 0)
    curl_ref[5] = along(1, 0) - along(0, 1)

    material = materials_ref[...]
    for m in range(2):
        base = jnp.zeros((1, ELEMS), f32)
        for k in range(MATS):
            base = jnp.where(material == k, table_ref[m, k], base)
        weight_ref[m] = jnp.zeros((32, ELEMS), f32)
        weight_ref[m, 0:QPTS, :] = profile_ref[:, m, :] * base
    curl_ref.send()
    weight_ref.send()

    pad_ref[0:32, :] = jnp.zeros((32, NP), f32)
    pad_ref[0:QPTS, :] = interp
    lifted = mm_exact(pad_ref[0:32, :], mm_exact(lift_ref[...], widen_ref[...]))
    high, low = high_low(lifted)
    column = lax.broadcasted_iota(jnp.int32, (32, 192), 1)
    lift_out_ref[...] = jnp.where(column < 128, high.astype(f32), low.astype(f32)).astype(bf16)
    projected = mm_exact(project_ref[...], widen_q_ref[...])
    high, low = high_low(projected)
    column = lax.broadcasted_iota(jnp.int32, (NP, 96), 1)
    project_out_ref[...] = jnp.where(column < 64, high.astype(f32), low.astype(f32)).astype(bf16)
    lift_out_ref.send()
    project_out_ref.send()

    for face in range(4):
        lanes = slice(face * ELEMS, (face + 1) * ELEMS)
        mate = partner_ref[face : face + 1, :]
        total = jnp.zeros((192, ELEMS), f32)
        for source in range(4):
            held = trace_ref[:, source * ELEMS : (source + 1) * ELEMS]
            total = total + mm(held, one_hot_rows(ELEMS, source * ELEMS, mate))
        outside = total[:96] + total[96:]
        own = trace_ref[:, lanes].astype(f32)
        inside = own[:96] + own[96:]
        skin = mate == lax.broadcasted_iota(jnp.int32, (1, ELEMS), 1) + face * ELEMS
        jump_ref[:48, lanes] = jnp.where(skin, -inside[:48], outside[:48]) - inside[:48]
        jump_ref[48:, lanes] = outside[48:] - inside[48:]
    jump_ref.send()


def late_kernel(
    below_ref,
    above_ref,
    partner_ref,
    jump_ref,
    normals_ref,
    scale_ref,
    curl_ref,
    weight_ref,
    lift_ref,
    project_ref,
    normal_pick_ref,
    fields_ref,
    res_ref,
    slots_ref,
    workers_ref,
    phase_time_ref,
    on_face_ref,
    spread_ref,
    dirs_ref,
    spectra_ref,
    phase_ref,
    fields_out,
    res_out,
    spectra_out,
    far_out,
    flux_ref,
    points_ref,
    nodal_ref,
    group_ref,
    far_ref,
):
    flux_ref[...] = jnp.zeros(flux_ref.shape, bf16)
    nodal_ref[...] = jnp.zeros(nodal_ref.shape, f32)

    below_high, below_low = high_low(below_ref[...])
    above_high, above_low = high_low(above_ref[...])
    below = jnp.concatenate([below_high, below_low], axis=0)
    above = jnp.concatenate([above_high, above_low], axis=0)
    for face in range(4):
        lanes = slice(face * ELEMS, (face + 1) * ELEMS)
        mate = partner_ref[face : face + 1, :]
        met = mm(below, one_hot_rows(SHARED, 4 * ELEMS, mate)) + mm(
            above, one_hot_rows(SHARED, 4 * ELEMS + SHARED, mate)
        )
        jump = jump_ref[:, lanes] + (met[:96] + met[96:])
        e = [jump[i * 16 : (i + 1) * 16] for i in range(3)]
        h = [jump[i * 16 : (i + 1) * 16] for i in range(3, 6)]
        n = [normals_ref[k, face : face + 1, :] for k in range(3)]
        half = 0.5 * scale_ref[face : face + 1, :]
        normal_e = n[0] * e[0] + n[1] * e[1] + n[2] * e[2]
        normal_h = n[0] * h[0] + n[1] * h[1] + n[2] * h[2]
        for i in range(3):
            a, b = (i + 1) % 3, (i + 2) % 3
            flux_e = (n[a] * h[b] - n[b] * h[a] + e[i] - normal_e * n[i]) * half
            flux_h = (n[b] * e[a] - n[a] * e[b] + h[i] - normal_h * n[i]) * half
            for c, flux in ((i, flux_e), (3 + i, flux_h)):
                high, low = high_low(flux)
                flux_ref[c, face * 16 : (face + 1) * 16, :] = high
                flux_ref[c, 64 + face * 16 : 64 + (face + 1) * 16, :] = low
                flux_ref[c, 128 + face * 16 : 128 + (face + 1) * 16, :] = high

    lift = lift_ref[...]
    project = project_ref[...]
    for c in range(6):
        values = (curl_ref[c] + mm(lift, flux_ref[c])) * weight_ref[c // 3]
        high, low = high_low(values)
        points_ref[c, 0:32, :] = high
        points_ref[c, 32:64, :] = low
        points_ref[c, 64:96, :] = high
        new_res = rk_alpha * res_ref[c] + time_step * mm(project, points_ref[c])
        res_out[c] = new_res
        new_fields = fields_ref[c] + rk_beta * new_res
        fields_out[c] = new_fields
        nodal_ref[c * 32 : c * 32 + NP, :] = new_fields
    fields_out.send()
    res_out.send()

    slots = slots_ref[...]
    pick = one_hot_rows(ELEMS, 0, slots & (ELEMS - 1))
    face_id = lax.shift_right_logical(slots, 9)
    high, low = high_low(nodal_ref[...])
    picked = mm(high, pick) + mm(low, pick)
    on_face = on_face_ref[...]
    mask = jnp.zeros((32, HDEV), f32)
    for face in range(4):
        mask = jnp.where(face_id == face, on_face[:, face : face + 1], mask)
    mean = [
        jnp.sum(picked[c * 32 : (c + 1) * 32] * mask, axis=0, keepdims=True) * (1.0 / NFP)
        for c in range(6)
    ]
    n = [normal_pick_ref[k : k + 1, :] for k in range(3)]
    electric, magnetic = mean[:3], mean[3:]
    current = []
    for sign, field in ((1.0, magnetic), (-1.0, electric)):
        for i in range(3):
            a, b = (i + 1) % 3, (i + 2) % 3
            current.append((n[a] * field[b] - n[b] * field[a]) * sign)

    cos_time, sin_time = cos_sin_turns(phase_time_ref[...] * (0.5 / math.pi))
    turn = (column_of(cos_time), column_of(sin_time))
    for i in range(12):
        updated = spectra_ref[i] + turn[i // 6] * current[i % 6]
        spectra_out[i] = updated
        for g in range(GROUPS):
            group_ref[g, i * 8 : (i + 1) * 8, :] = updated[g * 8 : (g + 1) * 8]

    spectra_out.send()

    workers = workers_ref[...].astype(f32)
    same = column_of(workers) == workers
    earlier = lax.broadcasted_iota(jnp.int32, (HDEV, HDEV), 0) < lax.broadcasted_iota(
        jnp.int32, (HDEV, HDEV), 1
    )
    rank = jnp.sum(jnp.where(same & earlier, 1.0, 0.0), axis=0, keepdims=True)
    target = (rank * GRP + workers).astype(jnp.int32)
    placing = one_hot_rows(GRP * CAP, 0, target)
    nt = (((1,), (1,)), ((), ()))
    high, low = high_low(spectra_out[...].reshape(12 * FREQS, HDEV))
    placed = lax.dot_general(placing, high, nt, preferred_element_type=f32) + lax.dot_general(
        placing, low, nt, preferred_element_type=f32
    )
    for j in range(3):
        far_out[pl.ds(CHUNK + j, MEMBERS, stride=ROWS), :] = placed[:, j * 128 : (j + 1) * 128]

    spread = spread_ref[...].astype(bf16)
    own = (lax.broadcasted_iota(jnp.int32, (192, 256), 0) & 7) == lax.shift_right_logical(
        lax.broadcasted_iota(jnp.int32, (192, 256), 1), 5
    )
    theta = [dirs_ref[3 + k : 4 + k, :] for k in range(3)]
    phi = [dirs_ref[6 + k : 7 + k, :] for k in range(2)]

    def onto_theta(v):
        return theta[0] * v[0] + theta[1] * v[1] + theta[2] * v[2]

    def onto_phi(v):
        return phi[0] * v[0] + phi[1] * v[1]

    for g in range(GROUPS):
        high, low = high_low(group_ref[g])
        rows = jnp.where(own, mm(jnp.concatenate([high, low], axis=0), spread), 0.0).astype(bf16)
        cos_sum = mm(rows, phase_ref[g, 0])
        cos_sum = cos_sum[:96] + (cos_sum[96:] + mm(rows[:96], phase_ref[g, 1]))
        sin_sum = mm(rows, phase_ref[g, 2])
        sin_sum = sin_sum[:96] + (sin_sum[96:] + mm(rows[:96], phase_ref[g, 3]))

        def at(values, i):
            return values[i * 8 : (i + 1) * 8]

        real = [at(cos_sum, i) - at(sin_sum, i + 6) for i in range(6)]
        imag = [at(sin_sum, i) + at(cos_sum, i + 6) for i in range(6)]
        parts = (
            onto_theta(real[:3]) + onto_phi(real[3:]),
            onto_theta(imag[:3]) + onto_phi(imag[3:]),
            onto_theta(real[3:]) - onto_phi(real[:3]),
            onto_theta(imag[3:]) - onto_phi(imag[:3]),
        )
        for c, part in enumerate(parts):
            far_ref[c * FREQS + g * 8 : c * FREQS + (g + 1) * 8, :] = part
    far = far_ref[...].T
    for r in range(CHUNK):
        far_out[pl.ds(r, MEMBERS, stride=ROWS), :] = far[r * MEMBERS : (r + 1) * MEMBERS]


def sum_kernel(arrived_ref, sum_ref, pieces_ref):
    rows = [
        jnp.sum(arrived_ref[pl.ds(r, MEMBERS, stride=ROWS), :], axis=0, keepdims=True) for r in range(CHUNK)
    ]
    total = jnp.concatenate(rows, axis=0)
    for z in range(sum_ref.shape[0]):
        sum_ref[z] = total
    for j in range(3):
        piece = arrived_ref[pl.ds(CHUNK + j, MEMBERS, stride=ROWS), :]
        pieces_ref[:, j] = piece.reshape(MEMBERS // GRP, GRP, 128)


def join_kernel(arrived_ref, pieces_ref, message_ref):
    total = jnp.sum(arrived_ref[...], axis=0)
    for p in range(message_ref.shape[0]):
        message_ref[p, 0] = total
        message_ref[p, 1:] = pieces_ref[p]


def final_kernel(arrived_ref, far_ref, worker_ref, rows_ref):
    for p in range(arrived_ref.shape[0]):
        far_ref[p * CHUNK : (p + 1) * CHUNK, :] = arrived_ref[p, 0]
        for j in range(3):
            rows_ref[j, pl.ds(p, GRP, stride=CAP), :] = arrived_ref[p, 1 + j]
    for j in range(3):
        worker_ref[4 * j : 4 * j + 4] = rows_ref[j].T.reshape(4, FREQS, GRP * CAP)


def sds(shape, dtype=f32):
    return jax.ShapeDtypeStruct(shape, dtype)


VMEM = pl.BlockSpec(memory_space=pltpu.VMEM)
SMEM = pl.BlockSpec(memory_space=pltpu.SMEM)
HBM = pl.BlockSpec(memory_space=pltpu.HBM)
WHOLE = 67043328


def factors(dom):
    return (dom // 8, 4, 2)


def per_device(
    fields,
    section_res,
    derivative,
    geometry,
    normals,
    face_scale,
    lift_matrix,
    interp_q,
    project_q,
    mat_table,
    materials,
    profile,
    face_partner,
    send_faces,
    spectra,
    huy_slots,
    huy_worker,
    huy_pos,
    wavenumber,
    time_phase,
    sizes,
):
    along_z, along_x, cores = sizes
    partitions = along_z * along_x * cores * GRP
    order = np.arange(DIRS).reshape(GRP, MEMBERS // GRP, CHUNK).transpose(2, 1, 0).reshape(-1)
    select, on_face, widen, widen_q, spread, directions = constants(
        order, 1.0 / math.sqrt(HDEV * partitions)
    )
    slots_row = huy_slots.reshape(1, HDEV)

    traces, lower, upper = call(
        trace_kernel,
        "traces",
        (fields, send_faces, select),
        0,
        3,
        (sds((192, 4 * ELEMS), bf16), sds((96, SHARED)), sds((96, SHARED))),
        1,
        [],
        WHOLE,
        2,
    )

    ring = ("z", "x", "core", "y")
    from_below = lax.ppermute(upper, ring, [(i, i + 1) for i in range(partitions - 1)])
    from_above = lax.ppermute(lower, ring, [(i + 1, i) for i in range(partitions - 1)])

    phases, jump, curl, weight, lift3, project3, normal_pick = call(
        early_kernel,
        "early",
        (
            wavenumber,
            mat_table,
            fields,
            face_partner,
            derivative,
            geometry,
            normals,
            interp_q,
            project_q,
            lift_matrix,
            materials.reshape(1, ELEMS),
            profile.transpose(1, 0, 2),
            slots_row,
            huy_pos,
            widen,
            widen_q,
            directions,
            traces,
        ),
        2,
        16,
        (
            sds((GROUPS, 4, 8 * HDEV, DIRS), bf16),
            sds((96, 4 * ELEMS)),
            sds((6, 32, ELEMS)),
            sds((2, 32, ELEMS)),
            sds((32, 192), bf16),
            sds((NP, 96), bf16),
            sds((8, HDEV)),
        ),
        7,
        [pltpu.VMEM((96, NP), f32), pltpu.VMEM((6, 96, ELEMS), f32)],
        WHOLE,
        10,
    )

    new_fields, new_res, spectra_t, message = call(
        late_kernel,
        "late",
        (
            from_below,
            from_above,
            face_partner,
            jump,
            normals,
            face_scale,
            curl,
            weight,
            lift3,
            project3,
            normal_pick,
            fields,
            section_res,
            slots_row,
            huy_worker.reshape(1, HDEV),
            time_phase.reshape(1, FREQS),
            on_face,
            spread,
            directions,
            spectra.transpose(1, 0, 2),
            phases,
        ),
        0,
        21,
        (
            sds((6, NP, ELEMS)),
            sds((6, NP, ELEMS)),
            sds((12, FREQS, HDEV)),
            sds((MEMBERS * ROWS, 4 * FREQS)),
        ),
        3,
        [
            pltpu.VMEM((6, 192, ELEMS), bf16),
            pltpu.VMEM((6, 96, ELEMS), bf16),
            pltpu.VMEM((192, ELEMS), f32),
            pltpu.VMEM((GROUPS, 96, HDEV), f32),
            pltpu.VMEM((4 * FREQS, DIRS), f32),
        ],
        WHOLE,
        8,
    )
    new_spectra = spectra_t.transpose(1, 0, 2)

    chunks = MEMBERS // GRP
    small = dict(compiler_params=pltpu.CompilerParams(vmem_limit_bytes=8 << 20))
    arrived = lax.all_to_all(
        message.reshape(MEMBERS, 1, ROWS * 128), ("x", "core", "y"), 0, 0, tiled=True
    ).reshape(MEMBERS * ROWS, 128)
    part, pieces = pl.pallas_call(
        sum_kernel,
        out_shape=(sds((along_z, CHUNK, 128)), sds((chunks, 3, GRP, 128))),
        in_specs=[VMEM],
        out_specs=(VMEM, VMEM),
        name="sum",
        **small,
    )(arrived)
    part = lax.all_to_all(part, "z", 0, 0, tiled=True)
    message = pl.pallas_call(
        join_kernel,
        out_shape=sds((chunks, 4, CHUNK, 128)),
        in_specs=[VMEM, VMEM],
        out_specs=VMEM,
        name="join",
        **small,
    )(part, pieces)
    arrived = lax.all_to_all(message, ("x", "core"), 0, 0, tiled=True)
    far_field, worker_t = pl.pallas_call(
        final_kernel,
        out_shape=(sds((chunks * CHUNK, 128)), sds((12, FREQS, GRP * CAP))),
        in_specs=[VMEM],
        out_specs=(VMEM, VMEM),
        scratch_shapes=[pltpu.VMEM((3, GRP * CAP, 128), f32)],
        name="final",
        **small,
    )(arrived)
    worker_spectra = worker_t.transpose(1, 0, 2)
    return (new_fields, new_res, new_spectra, worker_spectra, far_field)


def solution(mesh):
    dom = mesh.shape["dom"]
    sizes = factors(dom)
    fine = Mesh(mesh.devices.reshape(*sizes, GRP), ("z", "x", "core", "y"))
    every = ("z", "x", "core", "y")
    last = {1: P(every), 2: P(None, every), 3: P(None, None, every)}
    return jax.shard_map(
        lambda *args: per_device(*args, sizes=sizes),
        mesh=fine,
        in_specs=(
            last[3],
            last[3],
            P(),
            last[2],
            last[3],
            last[2],
            P(),
            P(),
            P(),
            P(),
            last[1],
            last[3],
            last[2],
            last[2],
            last[3],
            last[1],
            P(every, None),
            last[2],
            P(),
            P(),
        ),
        out_specs=(last[3], last[3], last[3], last[3], P("y", None)),
        check_vma=False,
    )
```

```python
import math

import jax
import jax.numpy as jnp
import numpy as np
from jax import lax
from jax.experimental import pallas as pl
from jax.experimental.pallas import tpu as pltpu
from jax.sharding import Mesh
from jax.sharding import PartitionSpec as P

CAP = 8
DIRS = 512
FREQS = 32
ELEMS = 512
HDEV = 32
SHARED = 128
NP = 20
NFP = 10
QPTS = 23
MATS = 6
GRP = 8
GROUPS = 4
CHUNK = 8
MEMBERS = 64
ROWS = CHUNK + 3

rk_alpha = -0.4178904745
rk_beta = 0.3792103129
time_step = 0.5
highest = lax.Precision.HIGHEST
f32 = jnp.float32
bf16 = jnp.bfloat16

COS_POLY = (
    1.4142134965648603,
    -6.97885098821926,
    5.73946117028719,
    -1.8835629847749262,
    0.3106981867542991,
)
SIN_POLY = (
    4.442882919199669,
    -7.308245696155,
    3.606354411402601,
    -0.8461128855994527,
    0.10982698719081677,
)
ROUNDER = 12582912.0


def face_nodes():
    lattice = [
        (along_a, along_b, along_c)
        for along_c in range(4)
        for along_b in range(4 - along_c)
        for along_a in range(4 - along_b - along_c)
    ]
    checkers = [
        lambda point_abc: point_abc[2] == 0,
        lambda point_abc: point_abc[1] == 0,
        lambda point_abc: sum(point_abc) == 3,
        lambda point_abc: point_abc[0] == 0,
    ]
    return np.array(
        [[n for n, abc in enumerate(lattice) if checker(abc)] for checker in checkers],
        dtype=np.int32,
    )


def constants(dir_order, norm_scale):
    nodes = face_nodes()
    on_face = np.zeros((32, 4), np.float32)
    widen = np.zeros((4 * NFP, 192), np.float32)
    for face in range(4):
        for j in range(NFP):
            on_face[nodes[face, j], face] = 1.0
            for copy in range(3):
                widen[face * NFP + j, copy * 64 + face * 16 + j] = 1.0
    widen_q = np.zeros((QPTS, 96), np.float32)
    for q in range(QPTS):
        for copy in range(3):
            widen_q[q, copy * 32 + q] = 1.0
    spread = np.zeros((HDEV, 8 * HDEV), np.float32)
    for h in range(HDEV):
        spread[h, h::HDEV] = 1.0
    row_ids = dir_order.astype(np.int64)
    height = 1.0 - (2.0 * row_ids + 1.0) / DIRS
    radius = np.sqrt(1.0 - height * height)
    azimuth = (row_ids * 381966 % 1000000) * 1e-06 * (2.0 * math.pi)
    cos_turn, sin_turn = np.cos(azimuth), np.sin(azimuth)
    zero = np.zeros_like(height)
    directions = np.stack(
        [radius * cos_turn, radius * sin_turn, height]
        + [norm_scale * v for v in (height * cos_turn, height * sin_turn, -radius)]
        + [norm_scale * v for v in (-sin_turn, cos_turn)]
        + [zero] * 8
    ).astype(np.float32)
    return on_face, widen, widen_q, spread, directions


def high_low(values):
    high = values.astype(bf16)
    return high, (values - high.astype(f32)).astype(bf16)


def mm(a, b):
    return jnp.dot(a, b, preferred_element_type=f32)


def mm_exact(a, b):
    return jnp.dot(a, b, preferred_element_type=f32, precision=highest)


def one_hot_rows(count, base, row):
    step = min(count, 256)
    ids = lax.broadcasted_iota(jnp.int32, (step, row.shape[1]), 0).astype(f32).astype(bf16)
    pieces = []
    for start in range(base, base + count, step):
        local = row - start
        local = jnp.where((local >= 0) & (local < step), local, -1).astype(f32).astype(bf16)
        pieces.append(jnp.where(ids == local, jnp.ones((), bf16), jnp.zeros((), bf16)))
    return pieces[0] if len(pieces) == 1 else jnp.concatenate(pieces, axis=0)


def cos_sin_turns(turns):
    part = turns - ((turns + ROUNDER) - ROUNDER)
    square = part * part
    cos_half = COS_POLY[-1] * square + COS_POLY[-2]
    sin_half = SIN_POLY[-1] * square + SIN_POLY[-2]
    for c, s in zip(COS_POLY[-3::-1], SIN_POLY[-3::-1]):
        cos_half = cos_half * square + c
        sin_half = sin_half * square + s
    sin_half = sin_half * part
    return 1.0 - sin_half * sin_half, sin_half * cos_half


def column_of(row):
    n = row.shape[1]
    eye = lax.broadcasted_iota(jnp.int32, (n, n), 0) == lax.broadcasted_iota(jnp.int32, (n, n), 1)
    return jnp.sum(jnp.where(eye, row, 0.0), axis=1, keepdims=True)


class Fetched:
    def __init__(self, source, target, sem):
        self.copy = pltpu.make_async_copy(source, target, sem)
        self.target = target
        self.waited = False
        self.copy.start()

    def ref(self):
        if not self.waited:
            self.copy.wait()
            self.waited = True
        return self.target

    def __getitem__(self, key):
        return self.ref()[key]


class Sent:
    def __init__(self, source, target, sem):
        self.source, self.target, self.sem = source, target, sem
        self.copies = []

    def __getitem__(self, key):
        return self.source[key]

    def __setitem__(self, key, value):
        self.source[key] = value

    @property
    def shape(self):
        return self.source.shape

    def send(self, *index):
        source, target = self.source, self.target
        if index:
            source, target = source.at[index], target.at[index]
        sem = self.sem.at[len(self.copies)]
        self.copies.append(pltpu.make_async_copy(source, target, sem))
        self.copies[-1].start()


def moving(kernel, first, fetched, n_in, sent, n_out):
    def wrapped(*refs):
        ins, outs, rest = refs[:n_in], refs[n_in : n_in + n_out], refs[n_in + n_out :]
        held = []
        if fetched:
            targets, sems, rest = rest[:fetched], rest[fetched], rest[fetched + 1 :]
            held = [Fetched(ins[first + i], targets[i], sems.at[i]) for i in range(fetched)]
        going = []
        if sent:
            sources, sems, rest = rest[:sent], rest[sent], rest[sent + 1 :]
            going = [Sent(sources[i], outs[i], sems.at[i]) for i in range(sent)]
        kernel(*ins[:first], *held, *ins[first + fetched :], *going, *outs[sent:], *rest)
        for one in held:
            one.ref()
        for one in going:
            for copy in one.copies:
                copy.wait()

    return wrapped


def call(kernel, name, operands, first, fetched, outs, sent, scratch, limit, micros):
    moved = operands[first : first + fetched]
    scratch_shapes = [pltpu.VMEM(a.shape, a.dtype) for a in moved]
    if fetched:
        scratch_shapes.append(pltpu.SemaphoreType.DMA((fetched,)))
    if sent:
        scratch_shapes += [pltpu.VMEM(o.shape, o.dtype) for o in outs[:sent]]
        scratch_shapes.append(pltpu.SemaphoreType.DMA((sent, GROUPS)))
    return pl.pallas_call(
        moving(kernel, first, fetched, len(operands), sent, len(outs)),
        out_shape=tuple(outs),
        in_specs=[SMEM] * first + [HBM] * fetched + [VMEM] * (len(operands) - first - fetched),
        out_specs=tuple([HBM] * sent + [VMEM] * (len(outs) - sent)),
        scratch_shapes=scratch_shapes + scratch,
        cost_estimate=pl.CostEstimate(flops=int(micros * 1.15e9), bytes_accessed=4 << 20, transcendentals=0),
        compiler_params=pltpu.CompilerParams(vmem_limit_bytes=limit),
        name=name,
    )(*operands)


def trace_kernel(fields_ref, send_ref, trace_ref, lower_ref, upper_ref):
    where = lax.broadcasted_iota(jnp.int32, (64, NP), 0) * 32 + lax.broadcasted_iota(
        jnp.int32, (64, NP), 1
    )
    chosen = jnp.zeros((64, NP), f32)
    for face, row in enumerate(face_nodes()):
        for j, node in enumerate(row):
            chosen = jnp.where(where == (face * 16 + j) * 32 + int(node), 1.0, chosen)
    select = chosen.astype(bf16)
    for c in range(6):
        for part, half in enumerate(high_low(fields_ref[c])):
            picked = mm(select, half).astype(bf16)
            for face in range(4):
                trace_ref[part * 96 + c * 16 : part * 96 + (c + 1) * 16, face * ELEMS : (face + 1) * ELEMS] = picked[
                    face * 16 : (face + 1) * 16
                ]
    send = send_ref[...]
    total = [jnp.zeros((192, SHARED), f32), jnp.zeros((192, SHARED), f32)]
    for face in range(4):
        held = trace_ref[:, face * ELEMS : (face + 1) * ELEMS]
        for row in range(2):
            total[row] = total[row] + mm(held, one_hot_rows(ELEMS, face * ELEMS, send[row : row + 1]))
    lower_ref[...] = total[0][:96] + total[0][96:]
    upper_ref[...] = total[1][:96] + total[1][96:]


def early_kernel(
    wave_ref,
    table_ref,
    fields_ref,
    partner_ref,
    derivative_ref,
    geometry_ref,
    normals_ref,
    interp_ref,
    project_ref,
    lift_ref,
    materials_ref,
    profile_ref,
    slots_ref,
    pos_ref,
    widen_ref,
    widen_q_ref,
    dirs_ref,
    trace_ref,
    phase_ref,
    jump_ref,
    curl_ref,
    weight_ref,
    lift_out_ref,
    project_out_ref,
    normal_out_ref,
    pad_ref,
    grad_ref,
):
    heading = dirs_ref[...]
    pos = pos_ref[...]
    path = jnp.zeros((HDEV, DIRS), f32)
    for k in range(3):
        path = path + column_of(pos[k : k + 1]) * heading[k : k + 1]
    for f in range(FREQS):
        cos_part, sin_part = cos_sin_turns(path * (wave_ref[f] * (0.5 / math.pi)))
        rows = slice((f % 8) * HDEV, (f % 8 + 1) * HDEV)
        for place, half in enumerate(high_low(cos_part) + high_low(sin_part)):
            phase_ref[f // 8, place, rows, :] = half

    slots = slots_ref[...]
    pick = one_hot_rows(ELEMS, 0, slots & (ELEMS - 1))
    face_id = lax.shift_right_logical(slots, 9)
    match = lax.broadcasted_iota(jnp.int32, (4, HDEV), 0) == face_id
    normal_out_ref[...] = jnp.zeros((8, HDEV), f32)
    for k in range(3):
        high, low = high_low(normals_ref[k])
        normal_out_ref[k : k + 1, :] = jnp.sum(
            jnp.where(match, mm(high, pick) + mm(low, pick), 0.0), axis=0, keepdims=True
        )

    interp = interp_ref[...]
    pad_ref[...] = jnp.zeros((96, NP), f32)
    for r in range(3):
        pad_ref[r * 32 : r * 32 + QPTS, :] = mm_exact(interp, derivative_ref[r])
    slope_high, slope_low = high_low(pad_ref[...])
    for c in range(6):
        high, low = high_low(fields_ref[c])
        grad_ref[c] = mm(slope_high, high) + (mm(slope_low, high) + mm(slope_high, low))

    def along(k, c):
        return (
            geometry_ref[k : k + 1, :] * grad_ref[c, 0:32, :]
            + geometry_ref[3 + k : 4 + k, :] * grad_ref[c, 32:64, :]
            + geometry_ref[6 + k : 7 + k, :] * grad_ref[c, 64:96, :]
        )

    curl_ref[0] = along(1, 5) - along(2, 4)
    curl_ref[1] = along(2, 3) - along(0, 5)
    curl_ref[2] = along(0, 4) - along(1, 3)
    curl_ref[3] = along(2, 1) - along(1, 2)
    curl_ref[4] = along(0, 2) - along(2, 0)
    curl_ref[5] = along(1, 0) - along(0, 1)

    material = materials_ref[...]
    for m in range(2):
        base = jnp.zeros((1, ELEMS), f32)
        for k in range(MATS):
            base = jnp.where(material == k, table_ref[m, k], base)
        weight_ref[m] = jnp.zeros((32, ELEMS), f32)
        weight_ref[m, 0:QPTS, :] = profile_ref[:, m, :] * base

    pad_ref[0:32, :] = jnp.zeros((32, NP), f32)
    pad_ref[0:QPTS, :] = interp
    lifted = mm_exact(pad_ref[0:32, :], mm_exact(lift_ref[...], widen_ref[...]))
    high, low = high_low(lifted)
    column = lax.broadcasted_iota(jnp.int32, (32, 192), 1)
    lift_out_ref[...] = jnp.where(column < 128, high.astype(f32), low.astype(f32)).astype(bf16)
    projected = mm_exact(project_ref[...], widen_q_ref[...])
    high, low = high_low(projected)
    column = lax.broadcasted_iota(jnp.int32, (NP, 96), 1)
    project_out_ref[...] = jnp.where(column < 64, high.astype(f32), low.astype(f32)).astype(bf16)

    for face in range(4):
        lanes = slice(face * ELEMS, (face + 1) * ELEMS)
        mate = partner_ref[face : face + 1, :]
        total = jnp.zeros((192, ELEMS), f32)
        for source in range(4):
            held = trace_ref[:, source * ELEMS : (source + 1) * ELEMS]
            total = total + mm(held, one_hot_rows(ELEMS, source * ELEMS, mate))
        outside = total[:96] + total[96:]
        own = trace_ref[:, lanes].astype(f32)
        inside = own[:96] + own[96:]
        skin = mate == lax.broadcasted_iota(jnp.int32, (1, ELEMS), 1) + face * ELEMS
        jump_ref[:48, lanes] = jnp.where(skin, -inside[:48], outside[:48]) - inside[:48]
        jump_ref[48:, lanes] = outside[48:] - inside[48:]


def late_kernel(
    below_ref,
    above_ref,
    partner_ref,
    jump_ref,
    normals_ref,
    scale_ref,
    curl_ref,
    weight_ref,
    lift_ref,
    project_ref,
    normal_pick_ref,
    fields_ref,
    res_ref,
    slots_ref,
    workers_ref,
    phase_time_ref,
    on_face_ref,
    spread_ref,
    dirs_ref,
    spectra_ref,
    phase_ref,
    fields_out,
    res_out,
    spectra_out,
    far_out,
    flux_ref,
    points_ref,
    nodal_ref,
    group_ref,
    far_ref,
):
    flux_ref[...] = jnp.zeros(flux_ref.shape, bf16)
    nodal_ref[...] = jnp.zeros(nodal_ref.shape, f32)

    below_high, below_low = high_low(below_ref[...])
    above_high, above_low = high_low(above_ref[...])
    below = jnp.concatenate([below_high, below_low], axis=0)
    above = jnp.concatenate([above_high, above_low], axis=0)
    for face in range(4):
        lanes = slice(face * ELEMS, (face + 1) * ELEMS)
        mate = partner_ref[face : face + 1, :]
        met = mm(below, one_hot_rows(SHARED, 4 * ELEMS, mate)) + mm(
            above, one_hot_rows(SHARED, 4 * ELEMS + SHARED, mate)
        )
        jump = jump_ref[:, lanes] + (met[:96] + met[96:])
        e = [jump[i * 16 : (i + 1) * 16] for i in range(3)]
        h = [jump[i * 16 : (i + 1) * 16] for i in range(3, 6)]
        n = [normals_ref[k, face : face + 1, :] for k in range(3)]
        half = 0.5 * scale_ref[face : face + 1, :]
        normal_e = n[0] * e[0] + n[1] * e[1] + n[2] * e[2]
        normal_h = n[0] * h[0] + n[1] * h[1] + n[2] * h[2]
        for i in range(3):
            a, b = (i + 1) % 3, (i + 2) % 3
            flux_e = (n[a] * h[b] - n[b] * h[a] + e[i] - normal_e * n[i]) * half
            flux_h = (n[b] * e[a] - n[a] * e[b] + h[i] - normal_h * n[i]) * half
            for c, flux in ((i, flux_e), (3 + i, flux_h)):
                high, low = high_low(flux)
                flux_ref[c, face * 16 : (face + 1) * 16, :] = high
                flux_ref[c, 64 + face * 16 : 64 + (face + 1) * 16, :] = low
                flux_ref[c, 128 + face * 16 : 128 + (face + 1) * 16, :] = high

    lift = lift_ref[...]
    project = project_ref[...]
    for c in range(6):
        values = (curl_ref[c] + mm(lift, flux_ref[c])) * weight_ref[c // 3]
        high, low = high_low(values)
        points_ref[c, 0:32, :] = high
        points_ref[c, 32:64, :] = low
        points_ref[c, 64:96, :] = high
        new_res = rk_alpha * res_ref[c] + time_step * mm(project, points_ref[c])
        res_out[c] = new_res
        new_fields = fields_ref[c] + rk_beta * new_res
        fields_out[c] = new_fields
        nodal_ref[c * 32 : c * 32 + NP, :] = new_fields
    fields_out.send()
    res_out.send()

    slots = slots_ref[...]
    pick = one_hot_rows(ELEMS, 0, slots & (ELEMS - 1))
    face_id = lax.shift_right_logical(slots, 9)
    high, low = high_low(nodal_ref[...])
    picked = mm(high, pick) + mm(low, pick)
    on_face = on_face_ref[...]
    mask = jnp.zeros((32, HDEV), f32)
    for face in range(4):
        mask = jnp.where(face_id == face, on_face[:, face : face + 1], mask)
    mean = [
        jnp.sum(picked[c * 32 : (c + 1) * 32] * mask, axis=0, keepdims=True) * (1.0 / NFP)
        for c in range(6)
    ]
    n = [normal_pick_ref[k : k + 1, :] for k in range(3)]
    electric, magnetic = mean[:3], mean[3:]
    current = []
    for sign, field in ((1.0, magnetic), (-1.0, electric)):
        for i in range(3):
            a, b = (i + 1) % 3, (i + 2) % 3
            current.append((n[a] * field[b] - n[b] * field[a]) * sign)

    cos_time, sin_time = cos_sin_turns(phase_time_ref[...] * (0.5 / math.pi))
    turn = (column_of(cos_time), column_of(sin_time))
    for i in range(12):
        updated = spectra_ref[i] + turn[i // 6] * current[i % 6]
        spectra_out[i] = updated
        for g in range(GROUPS):
            group_ref[g, i * 8 : (i + 1) * 8, :] = updated[g * 8 : (g + 1) * 8]

    spectra_out.send()

    workers = workers_ref[...].astype(f32)
    same = column_of(workers) == workers
    earlier = lax.broadcasted_iota(jnp.int32, (HDEV, HDEV), 0) < lax.broadcasted_iota(
        jnp.int32, (HDEV, HDEV), 1
    )
    rank = jnp.sum(jnp.where(same & earlier, 1.0, 0.0), axis=0, keepdims=True)
    target = (rank * GRP + workers).astype(jnp.int32)
    placing = one_hot_rows(GRP * CAP, 0, target)
    nt = (((1,), (1,)), ((), ()))
    high, low = high_low(spectra_out[...].reshape(12 * FREQS, HDEV))
    placed = lax.dot_general(placing, high, nt, preferred_element_type=f32) + lax.dot_general(
        placing, low, nt, preferred_element_type=f32
    )
    for j in range(3):
        far_out[pl.ds(CHUNK + j, MEMBERS, stride=ROWS), :] = placed[:, j * 128 : (j + 1) * 128]

    spread = spread_ref[...].astype(bf16)
    own = (lax.broadcasted_iota(jnp.int32, (192, 256), 0) & 7) == lax.shift_right_logical(
        lax.broadcasted_iota(jnp.int32, (192, 256), 1), 5
    )
    theta = [dirs_ref[3 + k : 4 + k, :] for k in range(3)]
    phi = [dirs_ref[6 + k : 7 + k, :] for k in range(2)]

    def onto_theta(v):
        return theta[0] * v[0] + theta[1] * v[1] + theta[2] * v[2]

    def onto_phi(v):
        return phi[0] * v[0] + phi[1] * v[1]

    for g in range(GROUPS):
        high, low = high_low(group_ref[g])
        rows = jnp.where(own, mm(jnp.concatenate([high, low], axis=0), spread), 0.0).astype(bf16)
        cos_sum = mm(rows, phase_ref[g, 0])
        cos_sum = cos_sum[:96] + (cos_sum[96:] + mm(rows[:96], phase_ref[g, 1]))
        sin_sum = mm(rows, phase_ref[g, 2])
        sin_sum = sin_sum[:96] + (sin_sum[96:] + mm(rows[:96], phase_ref[g, 3]))

        def at(values, i):
            return values[i * 8 : (i + 1) * 8]

        real = [at(cos_sum, i) - at(sin_sum, i + 6) for i in range(6)]
        imag = [at(sin_sum, i) + at(cos_sum, i + 6) for i in range(6)]
        parts = (
            onto_theta(real[:3]) + onto_phi(real[3:]),
            onto_theta(imag[:3]) + onto_phi(imag[3:]),
            onto_theta(real[3:]) - onto_phi(real[:3]),
            onto_theta(imag[3:]) - onto_phi(imag[:3]),
        )
        for c, part in enumerate(parts):
            far_ref[c * FREQS + g * 8 : c * FREQS + (g + 1) * 8, :] = part
    far = far_ref[...].T
    for r in range(CHUNK):
        far_out[pl.ds(r, MEMBERS, stride=ROWS), :] = far[r * MEMBERS : (r + 1) * MEMBERS]


def sum_kernel(arrived_ref, sum_ref, pieces_ref):
    rows = [
        jnp.sum(arrived_ref[pl.ds(r, MEMBERS, stride=ROWS), :], axis=0, keepdims=True) for r in range(CHUNK)
    ]
    total = jnp.concatenate(rows, axis=0)
    for z in range(sum_ref.shape[0]):
        sum_ref[z] = total
    for j in range(3):
        piece = arrived_ref[pl.ds(CHUNK + j, MEMBERS, stride=ROWS), :]
        pieces_ref[:, j] = piece.reshape(MEMBERS // GRP, GRP, 128)


def join_kernel(arrived_ref, pieces_ref, message_ref):
    total = jnp.sum(arrived_ref[...], axis=0)
    for p in range(message_ref.shape[0]):
        message_ref[p, 0] = total
        message_ref[p, 1:] = pieces_ref[p]


def final_kernel(arrived_ref, far_ref, worker_ref, rows_ref):
    for p in range(arrived_ref.shape[0]):
        far_ref[p * CHUNK : (p + 1) * CHUNK, :] = arrived_ref[p, 0]
        for j in range(3):
            rows_ref[j, pl.ds(p, GRP, stride=CAP), :] = arrived_ref[p, 1 + j]
    for j in range(3):
        worker_ref[4 * j : 4 * j + 4] = rows_ref[j].T.reshape(4, FREQS, GRP * CAP)


def sds(shape, dtype=f32):
    return jax.ShapeDtypeStruct(shape, dtype)


VMEM = pl.BlockSpec(memory_space=pltpu.VMEM)
SMEM = pl.BlockSpec(memory_space=pltpu.SMEM)
HBM = pl.BlockSpec(memory_space=pltpu.HBM)
WHOLE = 67043328
PART = 36 << 20


def factors(dom):
    return (dom // 8, 4, 2)


def per_device(
    fields,
    section_res,
    derivative,
    geometry,
    normals,
    face_scale,
    lift_matrix,
    interp_q,
    project_q,
    mat_table,
    materials,
    profile,
    face_partner,
    send_faces,
    spectra,
    huy_slots,
    huy_worker,
    huy_pos,
    wavenumber,
    time_phase,
    sizes,
):
    along_z, along_x, cores = sizes
    partitions = along_z * along_x * cores * GRP
    order = np.arange(DIRS).reshape(GRP, MEMBERS // GRP, CHUNK).transpose(2, 1, 0).reshape(-1)
    on_face, widen, widen_q, spread, directions = constants(
        order, 1.0 / math.sqrt(HDEV * partitions)
    )
    slots_row = huy_slots.reshape(1, HDEV)

    traces, lower, upper = call(
        trace_kernel,
        "traces",
        (fields, send_faces),
        0,
        0,
        (sds((192, 4 * ELEMS), bf16), sds((96, SHARED)), sds((96, SHARED))),
        0,
        [],
        PART,
        2,
    )

    ring = ("z", "x", "core", "y")
    from_below = lax.ppermute(upper, ring, [(i, i + 1) for i in range(partitions - 1)])
    from_above = lax.ppermute(lower, ring, [(i + 1, i) for i in range(partitions - 1)])

    phases, jump, curl, weight, lift3, project3, normal_pick = call(
        early_kernel,
        "early",
        (
            wavenumber,
            mat_table,
            fields,
            face_partner,
            derivative,
            geometry,
            normals,
            interp_q,
            project_q,
            lift_matrix,
            materials.reshape(1, ELEMS),
            profile.transpose(1, 0, 2),
            slots_row,
            huy_pos,
            widen,
            widen_q,
            directions,
            traces,
        ),
        2,
        0,
        (
            sds((GROUPS, 4, 8 * HDEV, DIRS), bf16),
            sds((96, 4 * ELEMS)),
            sds((6, 32, ELEMS)),
            sds((2, 32, ELEMS)),
            sds((32, 192), bf16),
            sds((NP, 96), bf16),
            sds((8, HDEV)),
        ),
        0,
        [pltpu.VMEM((96, NP), f32), pltpu.VMEM((6, 96, ELEMS), f32)],
        PART,
        10,
    )

    new_fields, new_res, spectra_t, message = call(
        late_kernel,
        "late",
        (
            from_below,
            from_above,
            face_partner,
            jump,
            normals,
            face_scale,
            curl,
            weight,
            lift3,
            project3,
            normal_pick,
            fields,
            section_res,
            slots_row,
            huy_worker.reshape(1, HDEV),
            time_phase.reshape(1, FREQS),
            on_face,
            spread,
            directions,
            spectra.transpose(1, 0, 2),
            phases,
        ),
        0,
        0,
        (
            sds((6, NP, ELEMS)),
            sds((6, NP, ELEMS)),
            sds((12, FREQS, HDEV)),
            sds((MEMBERS * ROWS, 4 * FREQS)),
        ),
        3,
        [
            pltpu.VMEM((6, 192, ELEMS), bf16),
            pltpu.VMEM((6, 96, ELEMS), bf16),
            pltpu.VMEM((192, ELEMS), f32),
            pltpu.VMEM((GROUPS, 96, HDEV), f32),
            pltpu.VMEM((4 * FREQS, DIRS), f32),
        ],
        PART,
        8,
    )
    new_spectra = spectra_t.transpose(1, 0, 2)

    chunks = MEMBERS // GRP
    small = dict(compiler_params=pltpu.CompilerParams(vmem_limit_bytes=8 << 20))
    arrived = lax.all_to_all(
        message.reshape(MEMBERS, 1, ROWS * 128), ("x", "core", "y"), 0, 0, tiled=True
    ).reshape(MEMBERS * ROWS, 128)
    part, pieces = pl.pallas_call(
        sum_kernel,
        out_shape=(sds((along_z, CHUNK, 128)), sds((chunks, 3, GRP, 128))),
        in_specs=[VMEM],
        out_specs=(VMEM, VMEM),
        name="sum",
        **small,
    )(arrived)
    part = lax.all_to_all(part, "z", 0, 0, tiled=True)
    message = pl.pallas_call(
        join_kernel,
        out_shape=sds((chunks, 4, CHUNK, 128)),
        in_specs=[VMEM, VMEM],
        out_specs=VMEM,
        name="join",
        **small,
    )(part, pieces)
    arrived = lax.all_to_all(message, ("x", "core"), 0, 0, tiled=True)
    far_field, worker_t = pl.pallas_call(
        final_kernel,
        out_shape=(sds((chunks * CHUNK, 128)), sds((12, FREQS, GRP * CAP))),
        in_specs=[VMEM],
        out_specs=(VMEM, VMEM),
        scratch_shapes=[pltpu.VMEM((3, GRP * CAP, 128), f32)],
        name="final",
        **small,
    )(arrived)
    worker_spectra = worker_t.transpose(1, 0, 2)
    return (new_fields, new_res, new_spectra, worker_spectra, far_field)


def solution(mesh):
    dom = mesh.shape["dom"]
    sizes = factors(dom)
    fine = Mesh(mesh.devices.reshape(*sizes, GRP), ("z", "x", "core", "y"))
    every = ("z", "x", "core", "y")
    last = {1: P(every), 2: P(None, every), 3: P(None, None, every)}
    return jax.shard_map(
        lambda *args: per_device(*args, sizes=sizes),
        mesh=fine,
        in_specs=(
            last[3],
            last[3],
            P(),
            last[2],
            last[3],
            last[2],
            P(),
            P(),
            P(),
            P(),
            last[1],
            last[3],
            last[2],
            last[2],
            last[3],
            last[1],
            P(every, None),
            last[2],
            P(),
            P(),
        ),
        out_specs=(last[3], last[3], last[3], last[3], P("y", None)),
        check_vma=False,
    )
```

```python
import math

import jax
import jax.numpy as jnp
import numpy as np
from jax import lax
from jax.experimental import pallas as pl
from jax.experimental.pallas import tpu as pltpu
from jax.sharding import Mesh
from jax.sharding import PartitionSpec as P

CAP = 8
DIRS = 512
FREQS = 32
ELEMS = 512
HDEV = 32
SHARED = 128
NP = 20
NFP = 10
QPTS = 23
MATS = 6
GRP = 8
GROUPS = 4
CHUNK = 8
MEMBERS = 64
ROWS = CHUNK + 3

rk_alpha = -0.4178904745
rk_beta = 0.3792103129
time_step = 0.5
highest = lax.Precision.HIGHEST
f32 = jnp.float32
bf16 = jnp.bfloat16

COS_POLY = (
    1.4142134965648603,
    -6.97885098821926,
    5.73946117028719,
    -1.8835629847749262,
    0.3106981867542991,
)
SIN_POLY = (
    4.442882919199669,
    -7.308245696155,
    3.606354411402601,
    -0.8461128855994527,
    0.10982698719081677,
)
ROUNDER = 12582912.0


def face_nodes():
    lattice = [
        (along_a, along_b, along_c)
        for along_c in range(4)
        for along_b in range(4 - along_c)
        for along_a in range(4 - along_b - along_c)
    ]
    checkers = [
        lambda point_abc: point_abc[2] == 0,
        lambda point_abc: point_abc[1] == 0,
        lambda point_abc: sum(point_abc) == 3,
        lambda point_abc: point_abc[0] == 0,
    ]
    return np.array(
        [[n for n, abc in enumerate(lattice) if checker(abc)] for checker in checkers],
        dtype=np.int32,
    )


def constants(dir_order, norm_scale):
    nodes = face_nodes()
    on_face = np.zeros((32, 4), np.float32)
    widen = np.zeros((4 * NFP, 192), np.float32)
    for face in range(4):
        for j in range(NFP):
            on_face[nodes[face, j], face] = 1.0
            for copy in range(3):
                widen[face * NFP + j, copy * 64 + face * 16 + j] = 1.0
    widen_q = np.zeros((QPTS, 96), np.float32)
    for q in range(QPTS):
        for copy in range(3):
            widen_q[q, copy * 32 + q] = 1.0
    spread = np.zeros((HDEV, 8 * HDEV), np.float32)
    for h in range(HDEV):
        spread[h, h::HDEV] = 1.0
    row_ids = dir_order.astype(np.int64)
    height = 1.0 - (2.0 * row_ids + 1.0) / DIRS
    radius = np.sqrt(1.0 - height * height)
    azimuth = (row_ids * 381966 % 1000000) * 1e-06 * (2.0 * math.pi)
    cos_turn, sin_turn = np.cos(azimuth), np.sin(azimuth)
    zero = np.zeros_like(height)
    directions = np.stack(
        [radius * cos_turn, radius * sin_turn, height]
        + [norm_scale * v for v in (height * cos_turn, height * sin_turn, -radius)]
        + [norm_scale * v for v in (-sin_turn, cos_turn)]
        + [zero] * 8
    ).astype(np.float32)
    return on_face, widen, widen_q, spread, directions


def high_low(values):
    high = values.astype(bf16)
    return high, (values - high.astype(f32)).astype(bf16)


def mm(a, b):
    return jnp.dot(a, b, preferred_element_type=f32)


def mm_exact(a, b):
    return jnp.dot(a, b, preferred_element_type=f32, precision=highest)


def one_hot_rows(count, base, row):
    step = min(count, 256)
    ids = lax.broadcasted_iota(jnp.int32, (step, row.shape[1]), 0).astype(f32).astype(bf16)
    pieces = []
    for start in range(base, base + count, step):
        local = row - start
        local = jnp.where((local >= 0) & (local < step), local, -1).astype(f32).astype(bf16)
        pieces.append(jnp.where(ids == local, jnp.ones((), bf16), jnp.zeros((), bf16)))
    return pieces[0] if len(pieces) == 1 else jnp.concatenate(pieces, axis=0)


def cos_sin_turns(turns):
    part = turns - ((turns + ROUNDER) - ROUNDER)
    square = part * part
    cos_half = COS_POLY[-1] * square + COS_POLY[-2]
    sin_half = SIN_POLY[-1] * square + SIN_POLY[-2]
    for c, s in zip(COS_POLY[-3::-1], SIN_POLY[-3::-1]):
        cos_half = cos_half * square + c
        sin_half = sin_half * square + s
    sin_half = sin_half * part
    return 1.0 - sin_half * sin_half, sin_half * cos_half


def column_of(row):
    n = row.shape[1]
    eye = lax.broadcasted_iota(jnp.int32, (n, n), 0) == lax.broadcasted_iota(jnp.int32, (n, n), 1)
    return jnp.sum(jnp.where(eye, row, 0.0), axis=1, keepdims=True)


class Fetched:
    def __init__(self, source, target, sem):
        self.copy = pltpu.make_async_copy(source, target, sem)
        self.target = target
        self.waited = False
        self.copy.start()

    def ref(self):
        if not self.waited:
            self.copy.wait()
            self.waited = True
        return self.target

    def __getitem__(self, key):
        return self.ref()[key]


class Sent:
    def __init__(self, source, target, sem):
        self.source, self.target, self.sem = source, target, sem
        self.copies = []

    def __getitem__(self, key):
        return self.source[key]

    def __setitem__(self, key, value):
        self.source[key] = value

    @property
    def shape(self):
        return self.source.shape

    def send(self, *index):
        source, target = self.source, self.target
        if index:
            source, target = source.at[index], target.at[index]
        sem = self.sem.at[len(self.copies)]
        self.copies.append(pltpu.make_async_copy(source, target, sem))
        self.copies[-1].start()


def moving(kernel, first, fetched, n_in, sent, n_out):
    def wrapped(*refs):
        ins, outs, rest = refs[:n_in], refs[n_in : n_in + n_out], refs[n_in + n_out :]
        held = []
        if fetched:
            targets, sems, rest = rest[:fetched], rest[fetched], rest[fetched + 1 :]
            held = [Fetched(ins[first + i], targets[i], sems.at[i]) for i in range(fetched)]
        going = []
        if sent:
            sources, sems, rest = rest[:sent], rest[sent], rest[sent + 1 :]
            going = [Sent(sources[i], outs[i], sems.at[i]) for i in range(sent)]
        kernel(*ins[:first], *held, *ins[first + fetched :], *going, *outs[sent:], *rest)
        for one in held:
            one.ref()
        for one in going:
            for copy in one.copies:
                copy.wait()

    return wrapped


def call(kernel, name, operands, first, fetched, outs, sent, scratch, limit, micros):
    moved = operands[first : first + fetched]
    scratch_shapes = [pltpu.VMEM(a.shape, a.dtype) for a in moved]
    if fetched:
        scratch_shapes.append(pltpu.SemaphoreType.DMA((fetched,)))
    if sent:
        scratch_shapes += [pltpu.VMEM(o.shape, o.dtype) for o in outs[:sent]]
        scratch_shapes.append(pltpu.SemaphoreType.DMA((sent, GROUPS)))
    return pl.pallas_call(
        moving(kernel, first, fetched, len(operands), sent, len(outs)),
        out_shape=tuple(outs),
        in_specs=[SMEM] * first + [HBM] * fetched + [VMEM] * (len(operands) - first - fetched),
        out_specs=tuple([HBM] * sent + [VMEM] * (len(outs) - sent)),
        scratch_shapes=scratch_shapes + scratch,
        cost_estimate=pl.CostEstimate(flops=int(micros * 1.15e9), bytes_accessed=4 << 20, transcendentals=0),
        compiler_params=pltpu.CompilerParams(vmem_limit_bytes=limit),
        name=name,
    )(*operands)


def trace_kernel(fields_ref, send_ref, trace_ref, lower_ref, upper_ref):
    where = lax.broadcasted_iota(jnp.int32, (64, NP), 0) * 32 + lax.broadcasted_iota(
        jnp.int32, (64, NP), 1
    )
    chosen = jnp.zeros((64, NP), f32)
    for face, row in enumerate(face_nodes()):
        for j, node in enumerate(row):
            chosen = jnp.where(where == (face * 16 + j) * 32 + int(node), 1.0, chosen)
    select = chosen.astype(bf16)
    for c in range(6):
        for part, half in enumerate(high_low(fields_ref[c])):
            picked = mm(select, half).astype(bf16)
            for face in range(4):
                trace_ref[part * 96 + c * 16 : part * 96 + (c + 1) * 16, face * ELEMS : (face + 1) * ELEMS] = picked[
                    face * 16 : (face + 1) * 16
                ]
    send = send_ref[...]
    total = [jnp.zeros((192, SHARED), f32), jnp.zeros((192, SHARED), f32)]
    for face in range(4):
        held = trace_ref[:, face * ELEMS : (face + 1) * ELEMS]
        for row in range(2):
            total[row] = total[row] + mm(held, one_hot_rows(ELEMS, face * ELEMS, send[row : row + 1]))
    lower_ref[...] = total[0][:96] + total[0][96:]
    upper_ref[...] = total[1][:96] + total[1][96:]


def lane_faces():
    return lax.shift_right_logical(lax.broadcasted_iota(jnp.int32, (1, 128), 1), 5)


def fold(values):
    row = lax.broadcasted_iota(jnp.int32, (128, 128), 0)
    column = lax.broadcasted_iota(jnp.int32, (128, 128), 1)
    same = jnp.where((row & (HDEV - 1)) == (column & (HDEV - 1)), 1.0, 0.0).astype(bf16)
    high, low = high_low(values)
    return mm(high, same) + mm(low, same)


def project_far(dirs_ref, real, imag):
    theta = [dirs_ref[3 + k : 4 + k, :] for k in range(3)]
    phi = [dirs_ref[6 + k : 7 + k, :] for k in range(2)]

    def onto_theta(v):
        return theta[0] * v[0] + theta[1] * v[1] + theta[2] * v[2]

    def onto_phi(v):
        return phi[0] * v[0] + phi[1] * v[1]

    return (
        onto_theta(real[:3]) + onto_phi(real[3:]),
        onto_theta(imag[:3]) + onto_phi(imag[3:]),
        onto_theta(real[3:]) - onto_phi(real[:3]),
        onto_theta(imag[3:]) - onto_phi(imag[:3]),
    )


def at(values, i):
    return values[i * 8 : (i + 1) * 8]


def own_frequency(rows):
    return (lax.broadcasted_iota(jnp.int32, (rows, 256), 0) & 7) == lax.shift_right_logical(
        lax.broadcasted_iota(jnp.int32, (rows, 256), 1), 5
    )


def fluxes(jump, n, half):
    e = [jump[i * 16 : (i + 1) * 16] for i in range(3)]
    h = [jump[i * 16 : (i + 1) * 16] for i in range(3, 6)]
    normal_e = n[0] * e[0] + n[1] * e[1] + n[2] * e[2]
    normal_h = n[0] * h[0] + n[1] * h[1] + n[2] * h[2]
    flux_e, flux_h = [], []
    for i in range(3):
        a, b = (i + 1) % 3, (i + 2) % 3
        flux_e.append((n[a] * h[b] - n[b] * h[a] + e[i] - normal_e * n[i]) * half)
        flux_h.append((n[b] * e[a] - n[a] * e[b] + h[i] - normal_h * n[i]) * half)
    return flux_e + flux_h


def curls(slope, field_of, metric_of):
    slope_high, slope_low = high_low(slope)
    grads = []
    for c in range(6):
        high, low = high_low(field_of(c))
        grads.append(mm(slope_high, high) + (mm(slope_low, high) + mm(slope_high, low)))

    def along(k, c):
        return (
            metric_of(k) * grads[c][0:32]
            + metric_of(3 + k) * grads[c][32:64]
            + metric_of(6 + k) * grads[c][64:96]
        )

    return [
        along(1, 5) - along(2, 4),
        along(2, 3) - along(0, 5),
        along(0, 4) - along(1, 3),
        along(2, 1) - along(1, 2),
        along(0, 2) - along(2, 0),
        along(1, 0) - along(0, 1),
    ]


def inverse_of(table_ref, m, material):
    base = jnp.zeros(material.shape, f32)
    for k in range(MATS):
        base = jnp.where(material == k, table_ref[m, k], base)
    return base


def halo_operands(below_ref, above_ref):
    below_high, below_low = high_low(below_ref[...])
    above_high, above_low = high_low(above_ref[...])
    return (
        jnp.concatenate([below_high, below_low], axis=0),
        jnp.concatenate([above_high, above_low], axis=0),
    )


def met_at_halo(below, above, mate):
    met = mm(below, one_hot_rows(SHARED, 4 * ELEMS, mate)) + mm(
        above, one_hot_rows(SHARED, 4 * ELEMS + SHARED, mate)
    )
    return met[:96] + met[96:]


def early_kernel(
    wave_ref,
    table_ref,
    fields_ref,
    res_ref,
    partner_ref,
    derivative_ref,
    geometry_ref,
    normals_ref,
    scale_ref,
    interp_ref,
    project_ref,
    lift_ref,
    materials_ref,
    profile_ref,
    slots_ref,
    pos_ref,
    widen_ref,
    widen_q_ref,
    dirs_ref,
    spread_ref,
    spectra_ref,
    trace_ref,
    phase_ref,
    far_ref,
    jump_ref,
    curl_ref,
    weight_ref,
    fields_out,
    res_out,
    rows_ref,
    lift_out_ref,
    project_out_ref,
    slope_ref,
    pad_ref,
    stack_ref,
    group_ref,
):
    heading = dirs_ref[...]
    pos = pos_ref[...]
    path = jnp.zeros((HDEV, DIRS), f32)
    for k in range(3):
        path = path + column_of(pos[k : k + 1]) * heading[k : k + 1]
    for f in range(FREQS):
        cos_part, sin_part = cos_sin_turns(path * (wave_ref[f] * (0.5 / math.pi)))
        rows = slice((f % 8) * HDEV, (f % 8 + 1) * HDEV)
        for place, half in enumerate(high_low(cos_part) + high_low(sin_part)):
            phase_ref[f // 8, place, rows, :] = half

    for i in range(12):
        came = spectra_ref[i]
        for g in range(GROUPS):
            group_ref[g, i * 8 : (i + 1) * 8, :] = came[g * 8 : (g + 1) * 8]
    spread = spread_ref[...].astype(bf16)
    own = own_frequency(192)
    for g in range(GROUPS):
        high, low = high_low(group_ref[g])
        rows = jnp.where(own, mm(jnp.concatenate([high, low], axis=0), spread), 0.0).astype(bf16)
        cos_sum = mm(rows, phase_ref[g, 0])
        cos_sum = cos_sum[:96] + (cos_sum[96:] + mm(rows[:96], phase_ref[g, 1]))
        sin_sum = mm(rows, phase_ref[g, 2])
        sin_sum = sin_sum[:96] + (sin_sum[96:] + mm(rows[:96], phase_ref[g, 3]))
        real = [at(cos_sum, i) - at(sin_sum, i + 6) for i in range(6)]
        imag = [at(sin_sum, i) + at(cos_sum, i + 6) for i in range(6)]
        for c, part in enumerate(project_far(dirs_ref, real, imag)):
            far_ref[c * FREQS + g * 8 : c * FREQS + (g + 1) * 8, :] = part

    lane_face = lane_faces()
    tile = jnp.where(
        (lax.broadcasted_iota(jnp.int32, (HDEV, 128), 1) & (HDEV - 1))
        == lax.broadcasted_iota(jnp.int32, (HDEV, 128), 0),
        1.0,
        0.0,
    )
    slots = mm_exact(jnp.broadcast_to(slots_ref[...].astype(f32), (8, HDEV)), tile)[0:1]
    slots = (slots + 0.5).astype(jnp.int32)
    element = slots & (ELEMS - 1)
    face_id = lax.shift_right_logical(slots, 9)
    pick = one_hot_rows(ELEMS, 0, element)

    def take(values):
        high, low = high_low(values)
        return mm(high, pick) + mm(low, pick)

    stack_ref[...] = jnp.zeros(stack_ref.shape, f32)
    for k in range(3):
        stack_ref[4 * k : 4 * k + 4, :] = normals_ref[k]
    stack_ref[12:16, :] = scale_ref[...]
    stack_ref[16:20, :] = partner_ref[...].astype(f32)
    stack_ref[24:33, :] = geometry_ref[...]
    stack_ref[33:34, :] = materials_ref[...].astype(f32)
    taken = take(stack_ref[...])

    def by_face(first):
        one = lax.broadcasted_iota(jnp.int32, (4, 128), 0) == lane_face
        return jnp.sum(jnp.where(one, taken[first : first + 4], 0.0), axis=0, keepdims=True)

    normal = [by_face(4 * k) for k in range(3)]
    mate_row = by_face(16)
    mate = (mate_row + 0.5).astype(jnp.int32)
    material = (taken[33:34] + 0.5).astype(jnp.int32)
    rows_ref[...] = jnp.zeros(rows_ref.shape, f32)
    for k in range(3):
        rows_ref[k : k + 1, :] = normal[k]
        rows_ref[8 + k : 9 + k, :] = jnp.where(lane_face == face_id, normal[k], 0.0)
    rows_ref[8:16, :] = fold(rows_ref[8:16, :])
    rows_ref[3:4, :] = 0.5 * by_face(12)
    rows_ref[4:5, :] = mate_row
    rows_ref[5:6, :] = face_id.astype(f32)
    for c in range(6):
        fields_out[c] = take(fields_ref[c])
        res_out[c] = take(res_ref[c])
    for m in range(2):
        weight_ref[m] = jnp.zeros((32, 128), f32)
        weight_ref[m, 0:QPTS, :] = take(profile_ref[:, m, :]) * inverse_of(table_ref, m, material)

    interp = interp_ref[...]
    slope_ref[...] = jnp.zeros((96, NP), f32)
    for r in range(3):
        slope_ref[r * 32 : r * 32 + QPTS, :] = mm_exact(interp, derivative_ref[r])
    for c, curl in enumerate(
        curls(slope_ref[...], lambda c: fields_out[c], lambda k: taken[24 + k : 25 + k])
    ):
        curl_ref[c] = curl

    inside = jnp.zeros((192, 128), f32)
    outside = jnp.zeros((192, 128), f32)
    for face in range(4):
        held = trace_ref[:, face * ELEMS : (face + 1) * ELEMS]
        inside = inside + jnp.where(lane_face == face, mm(held, pick), 0.0)
        outside = outside + mm(held, one_hot_rows(ELEMS, face * ELEMS, mate))
    inside = inside[:96] + inside[96:]
    outside = outside[:96] + outside[96:]
    skin = mate == lane_face * ELEMS + element
    jump_ref[:48, :] = jnp.where(skin, -inside[:48], outside[:48]) - inside[:48]
    jump_ref[48:, :] = outside[48:] - inside[48:]

    pad_ref[...] = jnp.zeros((32, NP), f32)
    pad_ref[0:QPTS, :] = interp
    lifted = mm_exact(pad_ref[...], mm_exact(lift_ref[...], widen_ref[...]))
    high, low = high_low(lifted)
    column = lax.broadcasted_iota(jnp.int32, (32, 192), 1)
    lift_out_ref[...] = jnp.where(column < 128, high.astype(f32), low.astype(f32)).astype(bf16)
    projected = mm_exact(project_ref[...], widen_q_ref[...])
    high, low = high_low(projected)
    column = lax.broadcasted_iota(jnp.int32, (NP, 96), 1)
    project_out_ref[...] = jnp.where(column < 64, high.astype(f32), low.astype(f32)).astype(bf16)


def late_kernel(
    below_ref,
    above_ref,
    rows_ref,
    jump_ref,
    curl_ref,
    weight_ref,
    lift_ref,
    project_ref,
    fields_ref,
    res_ref,
    workers_ref,
    phase_time_ref,
    on_face_ref,
    spread_ref,
    dirs_ref,
    spectra_ref,
    phase_ref,
    came_ref,
    spectra_out,
    far_out,
    current_out,
    flux_ref,
    lifted_ref,
    points_ref,
    far_ref,
):
    lane_face = lane_faces()
    below, above = halo_operands(below_ref, above_ref)
    mate = (rows_ref[4:5, :] + 0.5).astype(jnp.int32)
    jump = jump_ref[...] + met_at_halo(below, above, mate)
    normal = [rows_ref[k : k + 1, :] for k in range(3)]
    for c, flux in enumerate(fluxes(jump, normal, rows_ref[3:4, :])):
        lanes = slice(c * 128, (c + 1) * 128)
        for face in range(4):
            high, low = high_low(jnp.where(lane_face == face, flux, 0.0))
            flux_ref[face * 16 : (face + 1) * 16, lanes] = high
            flux_ref[64 + face * 16 : 64 + (face + 1) * 16, lanes] = low
            flux_ref[128 + face * 16 : 128 + (face + 1) * 16, lanes] = high
    lifted = mm(lift_ref[...], flux_ref[...])
    for c in range(6):
        lifted_ref[c * 32 : (c + 1) * 32, :] = lifted[:, c * 128 : (c + 1) * 128]
    lifted_ref[...] = fold(lifted_ref[...])
    for c in range(6):
        lanes = slice(c * 128, (c + 1) * 128)
        values = (curl_ref[c] + lifted_ref[c * 32 : (c + 1) * 32, :]) * weight_ref[c // 3]
        high, low = high_low(values)
        points_ref[0:32, lanes] = high
        points_ref[32:64, lanes] = low
        points_ref[64:96, lanes] = high
    adjusted = mm(project_ref[...], points_ref[...])

    face_id = (rows_ref[5:6, :] + 0.5).astype(jnp.int32)
    on_face = on_face_ref[...]
    mask = jnp.zeros((NP, 128), f32)
    for face in range(4):
        mask = jnp.where(face_id == face, on_face[:NP, face : face + 1], mask)
    mean = []
    for c in range(6):
        new_res = rk_alpha * res_ref[c] + time_step * adjusted[:, c * 128 : (c + 1) * 128]
        new_fields = fields_ref[c] + rk_beta * new_res
        mean.append(jnp.sum(new_fields * mask, axis=0, keepdims=True) * (1.0 / NFP))
    n = [rows_ref[8 + k : 9 + k, :] for k in range(3)]
    current_out[...] = jnp.zeros(current_out.shape, f32)
    current = []
    for sign, field in ((1.0, mean[3:]), (-1.0, mean[:3])):
        for i in range(3):
            a, b = (i + 1) % 3, (i + 2) % 3
            row = ((n[a] * field[b] - n[b] * field[a]) * sign)[:, :HDEV]
            current_out[len(current) : len(current) + 1, :] = row
            current.append(row)

    cos_time, sin_time = cos_sin_turns(phase_time_ref[...] * (0.5 / math.pi))
    turn = (column_of(cos_time), column_of(sin_time))
    for i in range(12):
        spectra_out[i] = spectra_ref[i] + turn[i // 6] * current[i % 6]
    spectra_out.send()

    workers = workers_ref[...].astype(f32)
    same = column_of(workers) == workers
    earlier = lax.broadcasted_iota(jnp.int32, (HDEV, HDEV), 0) < lax.broadcasted_iota(
        jnp.int32, (HDEV, HDEV), 1
    )
    rank = jnp.sum(jnp.where(same & earlier, 1.0, 0.0), axis=0, keepdims=True)
    target = (rank * GRP + workers).astype(jnp.int32)
    placing = one_hot_rows(GRP * CAP, 0, target)
    nt = (((1,), (1,)), ((), ()))
    high, low = high_low(spectra_out[...].reshape(12 * FREQS, HDEV))
    placed = lax.dot_general(placing, high, nt, preferred_element_type=f32) + lax.dot_general(
        placing, low, nt, preferred_element_type=f32
    )
    for j in range(3):
        far_out[pl.ds(CHUNK + j, MEMBERS, stride=ROWS), :] = placed[:, j * 128 : (j + 1) * 128]

    high, low = high_low(current_out[...])
    tiled = mm(jnp.concatenate([high, low], axis=0), spread_ref[...].astype(bf16))
    own = own_frequency(8)
    rows = [jnp.where(own, tiled[i : i + 1], 0.0) for i in range(6)]
    rows += [jnp.where(own, tiled[8 + i : 9 + i], 0.0) for i in range(6)]
    rows = jnp.concatenate(rows, axis=0).astype(bf16)
    for g in range(GROUPS):
        cos_sum = mm(rows, phase_ref[g, 0])
        cos_sum = cos_sum[:48] + (cos_sum[48:] + mm(rows[:48], phase_ref[g, 1]))
        sin_sum = mm(rows, phase_ref[g, 2])
        sin_sum = sin_sum[:48] + (sin_sum[48:] + mm(rows[:48], phase_ref[g, 3]))
        cos_turn, sin_turn = at(turn[0], g), at(turn[1], g)
        real = [cos_turn * at(cos_sum, i) - sin_turn * at(sin_sum, i) for i in range(6)]
        imag = [cos_turn * at(sin_sum, i) + sin_turn * at(cos_sum, i) for i in range(6)]
        for c, part in enumerate(project_far(dirs_ref, real, imag)):
            rows_of = slice(c * FREQS + g * 8, c * FREQS + (g + 1) * 8)
            far_ref[rows_of, :] = came_ref[rows_of, :] + part
    far = far_ref[...].T
    for r in range(CHUNK):
        far_out[pl.ds(r, MEMBERS, stride=ROWS), :] = far[r * MEMBERS : (r + 1) * MEMBERS]


def bulk_kernel(
    table_ref,
    current_ref,
    below_ref,
    above_ref,
    fields_ref,
    res_ref,
    partner_ref,
    geometry_ref,
    normals_ref,
    scale_ref,
    materials_ref,
    profile_ref,
    trace_ref,
    lift_ref,
    project_ref,
    slope_ref,
    fields_out,
    res_out,
    mark_ref,
    flux_ref,
    points_ref,
    weight_ref,
):
    mark_ref[...] = current_ref[...]
    flux_ref[...] = jnp.zeros(flux_ref.shape, bf16)
    below, above = halo_operands(below_ref, above_ref)
    for face in range(4):
        lanes = slice(face * ELEMS, (face + 1) * ELEMS)
        mate = partner_ref[face : face + 1, :]
        total = jnp.zeros((192, ELEMS), f32)
        for source in range(4):
            held = trace_ref[:, source * ELEMS : (source + 1) * ELEMS]
            total = total + mm(held, one_hot_rows(ELEMS, source * ELEMS, mate))
        outside = total[:96] + total[96:] + met_at_halo(below, above, mate)
        own = trace_ref[:, lanes].astype(f32)
        inside = own[:96] + own[96:]
        skin = mate == lax.broadcasted_iota(jnp.int32, (1, ELEMS), 1) + face * ELEMS
        jump = jnp.concatenate(
            [jnp.where(skin, -inside[:48], outside[:48]) - inside[:48], outside[48:] - inside[48:]], axis=0
        )
        normal = [normals_ref[k, face : face + 1, :] for k in range(3)]
        half = 0.5 * scale_ref[face : face + 1, :]
        for c, flux in enumerate(fluxes(jump, normal, half)):
            high, low = high_low(flux)
            flux_ref[c, face * 16 : (face + 1) * 16, :] = high
            flux_ref[c, 64 + face * 16 : 64 + (face + 1) * 16, :] = low
            flux_ref[c, 128 + face * 16 : 128 + (face + 1) * 16, :] = high
    material = materials_ref[...]
    for m in range(2):
        weight_ref[m] = jnp.zeros((32, ELEMS), f32)
        weight_ref[m, 0:QPTS, :] = profile_ref[:, m, :] * inverse_of(table_ref, m, material)
    curl = curls(slope_ref[...], lambda c: fields_ref[c], lambda k: geometry_ref[k : k + 1, :])
    lift = lift_ref[...]
    project = project_ref[...]
    for c in range(6):
        values = (curl[c] + mm(lift, flux_ref[c])) * weight_ref[c // 3]
        high, low = high_low(values)
        points_ref[c, 0:32, :] = high
        points_ref[c, 32:64, :] = low
        points_ref[c, 64:96, :] = high
        new_res = rk_alpha * res_ref[c] + time_step * mm(project, points_ref[c])
        res_out[c] = new_res
        fields_out[c] = fields_ref[c] + rk_beta * new_res
    fields_out.send()
    res_out.send()


def sum_kernel(arrived_ref, mark_ref, sum_ref, pieces_ref):
    rows = [
        jnp.sum(arrived_ref[pl.ds(r, MEMBERS, stride=ROWS), :], axis=0, keepdims=True) for r in range(CHUNK)
    ]
    total = jnp.concatenate(rows, axis=0)
    for z in range(sum_ref.shape[0]):
        sum_ref[z] = total
    for j in range(3):
        piece = arrived_ref[pl.ds(CHUNK + j, MEMBERS, stride=ROWS), :]
        pieces_ref[:, j] = piece.reshape(MEMBERS // GRP, GRP, 128)


def join_kernel(arrived_ref, pieces_ref, message_ref):
    total = jnp.sum(arrived_ref[...], axis=0)
    for p in range(message_ref.shape[0]):
        message_ref[p, 0] = total
        message_ref[p, 1:] = pieces_ref[p]


def final_kernel(arrived_ref, far_ref, worker_ref, rows_ref):
    for p in range(arrived_ref.shape[0]):
        far_ref[p * CHUNK : (p + 1) * CHUNK, :] = arrived_ref[p, 0]
        for j in range(3):
            rows_ref[j, pl.ds(p, GRP, stride=CAP), :] = arrived_ref[p, 1 + j]
    for j in range(3):
        worker_ref[4 * j : 4 * j + 4] = rows_ref[j].T.reshape(4, FREQS, GRP * CAP)


def sds(shape, dtype=f32):
    return jax.ShapeDtypeStruct(shape, dtype)


VMEM = pl.BlockSpec(memory_space=pltpu.VMEM)
SMEM = pl.BlockSpec(memory_space=pltpu.SMEM)
HBM = pl.BlockSpec(memory_space=pltpu.HBM)
WHOLE = 67043328
PART = 36 << 20


def factors(dom):
    return (dom // 8, 4, 2)


def per_device(
    fields,
    section_res,
    derivative,
    geometry,
    normals,
    face_scale,
    lift_matrix,
    interp_q,
    project_q,
    mat_table,
    materials,
    profile,
    face_partner,
    send_faces,
    spectra,
    huy_slots,
    huy_worker,
    huy_pos,
    wavenumber,
    time_phase,
    sizes,
):
    along_z, along_x, cores = sizes
    partitions = along_z * along_x * cores * GRP
    order = np.arange(DIRS).reshape(GRP, MEMBERS // GRP, CHUNK).transpose(2, 1, 0).reshape(-1)
    on_face, widen, widen_q, spread, directions = constants(
        order, 1.0 / math.sqrt(HDEV * partitions)
    )
    slots_row = huy_slots.reshape(1, HDEV)

    traces, lower, upper = call(
        trace_kernel,
        "traces",
        (fields, send_faces),
        0,
        0,
        (sds((192, 4 * ELEMS), bf16), sds((96, SHARED)), sds((96, SHARED))),
        0,
        [],
        PART,
        2,
    )

    ring = ("z", "x", "core", "y")
    from_below = lax.ppermute(upper, ring, [(i, i + 1) for i in range(partitions - 1)])
    from_above = lax.ppermute(lower, ring, [(i + 1, i) for i in range(partitions - 1)])

    partner = face_partner
    material_row = materials.reshape(1, ELEMS)
    coating = profile.transpose(1, 0, 2)
    came = spectra.transpose(1, 0, 2)
    phases, far_came, jump, curl, weight, fields_at, res_at, rows, lift3, project3, slope = call(
        early_kernel,
        "early",
        (
            wavenumber,
            mat_table,
            fields,
            section_res,
            partner,
            derivative,
            geometry,
            normals,
            face_scale,
            interp_q,
            project_q,
            lift_matrix,
            material_row,
            coating,
            slots_row,
            huy_pos,
            widen,
            widen_q,
            directions,
            spread,
            came,
            traces,
        ),
        2,
        0,
        (
            sds((GROUPS, 4, 8 * HDEV, DIRS), bf16),
            sds((4 * FREQS, DIRS)),
            sds((96, 128)),
            sds((6, 32, 128)),
            sds((2, 32, 128)),
            sds((6, NP, 128)),
            sds((6, NP, 128)),
            sds((16, 128)),
            sds((32, 192), bf16),
            sds((NP, 96), bf16),
            sds((96, NP)),
        ),
        0,
        [pltpu.VMEM((32, NP), f32), pltpu.VMEM((40, ELEMS), f32), pltpu.VMEM((GROUPS, 96, HDEV), f32)],
        PART,
        6,
    )

    spectra_t, message, current = call(
        late_kernel,
        "late",
        (
            from_below,
            from_above,
            rows,
            jump,
            curl,
            weight,
            lift3,
            project3,
            fields_at,
            res_at,
            huy_worker.reshape(1, HDEV),
            time_phase.reshape(1, FREQS),
            on_face,
            spread,
            directions,
            came,
            phases,
            far_came,
        ),
        0,
        0,
        (sds((12, FREQS, HDEV)), sds((MEMBERS * ROWS, 4 * FREQS)), sds((8, HDEV))),
        1,
        [
            pltpu.VMEM((192, 768), bf16),
            pltpu.VMEM((192, 128), f32),
            pltpu.VMEM((96, 768), bf16),
            pltpu.VMEM((4 * FREQS, DIRS), f32),
        ],
        PART,
        3,
    )

    new_fields, new_res, mark = call(
        bulk_kernel,
        "bulk",
        (
            mat_table,
            current,
            from_below,
            from_above,
            fields,
            section_res,
            partner,
            geometry,
            normals,
            face_scale,
            material_row,
            coating,
            traces,
            lift3,
            project3,
            slope,
        ),
        1,
        0,
        (sds((6, NP, ELEMS)), sds((6, NP, ELEMS)), sds((8, HDEV))),
        2,
        [
            pltpu.VMEM((6, 192, ELEMS), bf16),
            pltpu.VMEM((6, 96, ELEMS), bf16),
            pltpu.VMEM((2, 32, ELEMS), f32),
        ],
        PART,
        6,
    )
    new_spectra = spectra_t.transpose(1, 0, 2)

    chunks = MEMBERS // GRP
    small = dict(compiler_params=pltpu.CompilerParams(vmem_limit_bytes=8 << 20))
    arrived = lax.all_to_all(
        message.reshape(MEMBERS, 1, ROWS * 128), ("x", "core", "y"), 0, 0, tiled=True
    ).reshape(MEMBERS * ROWS, 128)
    part, pieces = pl.pallas_call(
        sum_kernel,
        out_shape=(sds((along_z, CHUNK, 128)), sds((chunks, 3, GRP, 128))),
        in_specs=[VMEM, VMEM],
        out_specs=(VMEM, VMEM),
        name="sum",
        **small,
    )(arrived, mark)
    part = lax.all_to_all(part, "z", 0, 0, tiled=True)
    message = pl.pallas_call(
        join_kernel,
        out_shape=sds((chunks, 4, CHUNK, 128)),
        in_specs=[VMEM, VMEM],
        out_specs=VMEM,
        name="join",
        **small,
    )(part, pieces)
    arrived = lax.all_to_all(message, ("x", "core"), 0, 0, tiled=True)
    far_field, worker_t = pl.pallas_call(
        final_kernel,
        out_shape=(sds((chunks * CHUNK, 128)), sds((12, FREQS, GRP * CAP))),
        in_specs=[VMEM],
        out_specs=(VMEM, VMEM),
        scratch_shapes=[pltpu.VMEM((3, GRP * CAP, 128), f32)],
        name="final",
        **small,
    )(arrived)
    worker_spectra = worker_t.transpose(1, 0, 2)
    return (new_fields, new_res, new_spectra, worker_spectra, far_field)


def solution(mesh):
    dom = mesh.shape["dom"]
    sizes = factors(dom)
    fine = Mesh(mesh.devices.reshape(*sizes, GRP), ("z", "x", "core", "y"))
    every = ("z", "x", "core", "y")
    last = {1: P(every), 2: P(None, every), 3: P(None, None, every)}
    return jax.shard_map(
        lambda *args: per_device(*args, sizes=sizes),
        mesh=fine,
        in_specs=(
            last[3],
            last[3],
            P(),
            last[2],
            last[3],
            last[2],
            P(),
            P(),
            P(),
            P(),
            last[1],
            last[3],
            last[2],
            last[2],
            last[3],
            last[1],
            P(every, None),
            last[2],
            P(),
            P(),
        ),
        out_specs=(last[3], last[3], last[3], last[3], P("y", None)),
        check_vma=False,
    )
```

```python
import math

import jax
import jax.numpy as jnp
import numpy as np
from jax import lax
from jax.experimental import pallas as pl
from jax.experimental.pallas import tpu as pltpu
from jax.sharding import Mesh
from jax.sharding import PartitionSpec as P

CAP = 8
DIRS = 512
FREQS = 32
ELEMS = 512
HDEV = 32
SHARED = 128
NP = 20
NFP = 10
QPTS = 23
MATS = 6
GRP = 8
GROUPS = 4
CHUNK = 8
MEMBERS = 64
ROWS = CHUNK + 3

rk_alpha = -0.4178904745
rk_beta = 0.3792103129
time_step = 0.5
highest = lax.Precision.HIGHEST
f32 = jnp.float32
bf16 = jnp.bfloat16

COS_POLY = (
    1.4142134965648603,
    -6.97885098821926,
    5.73946117028719,
    -1.8835629847749262,
    0.3106981867542991,
)
SIN_POLY = (
    4.442882919199669,
    -7.308245696155,
    3.606354411402601,
    -0.8461128855994527,
    0.10982698719081677,
)
ROUNDER = 12582912.0


def face_nodes():
    lattice = [
        (along_a, along_b, along_c)
        for along_c in range(4)
        for along_b in range(4 - along_c)
        for along_a in range(4 - along_b - along_c)
    ]
    checkers = [
        lambda point_abc: point_abc[2] == 0,
        lambda point_abc: point_abc[1] == 0,
        lambda point_abc: sum(point_abc) == 3,
        lambda point_abc: point_abc[0] == 0,
    ]
    return np.array(
        [[n for n, abc in enumerate(lattice) if checker(abc)] for checker in checkers],
        dtype=np.int32,
    )


def constants(dir_order, norm_scale):
    nodes = face_nodes()
    on_face = np.zeros((32, 4), np.float32)
    widen = np.zeros((4 * NFP, 192), np.float32)
    for face in range(4):
        for j in range(NFP):
            on_face[nodes[face, j], face] = 1.0
            for copy in range(3):
                widen[face * NFP + j, copy * 64 + face * 16 + j] = 1.0
    widen_q = np.zeros((QPTS, 96), np.float32)
    for q in range(QPTS):
        for copy in range(3):
            widen_q[q, copy * 32 + q] = 1.0
    spread = np.zeros((HDEV, 8 * HDEV), np.float32)
    for h in range(HDEV):
        spread[h, h::HDEV] = 1.0
    row_ids = dir_order.astype(np.int64)
    height = 1.0 - (2.0 * row_ids + 1.0) / DIRS
    radius = np.sqrt(1.0 - height * height)
    azimuth = (row_ids * 381966 % 1000000) * 1e-06 * (2.0 * math.pi)
    cos_turn, sin_turn = np.cos(azimuth), np.sin(azimuth)
    zero = np.zeros_like(height)
    directions = np.stack(
        [radius * cos_turn, radius * sin_turn, height]
        + [norm_scale * v for v in (height * cos_turn, height * sin_turn, -radius)]
        + [norm_scale * v for v in (-sin_turn, cos_turn)]
        + [zero] * 8
    ).astype(np.float32)
    return on_face, widen, widen_q, spread, directions


def high_low(values):
    high = values.astype(bf16)
    return high, (values - high.astype(f32)).astype(bf16)


def mm(a, b):
    return jnp.dot(a, b, preferred_element_type=f32)


def mm_exact(a, b):
    return jnp.dot(a, b, preferred_element_type=f32, precision=highest)


def one_hot_rows(count, base, row):
    step = min(count, 256)
    ids = lax.broadcasted_iota(jnp.int32, (step, row.shape[1]), 0).astype(f32).astype(bf16)
    pieces = []
    for start in range(base, base + count, step):
        local = row - start
        local = jnp.where((local >= 0) & (local < step), local, -1).astype(f32).astype(bf16)
        pieces.append(jnp.where(ids == local, jnp.ones((), bf16), jnp.zeros((), bf16)))
    return pieces[0] if len(pieces) == 1 else jnp.concatenate(pieces, axis=0)


def cos_sin_turns(turns):
    part = turns - ((turns + ROUNDER) - ROUNDER)
    square = part * part
    cos_half = COS_POLY[-1] * square + COS_POLY[-2]
    sin_half = SIN_POLY[-1] * square + SIN_POLY[-2]
    for c, s in zip(COS_POLY[-3::-1], SIN_POLY[-3::-1]):
        cos_half = cos_half * square + c
        sin_half = sin_half * square + s
    sin_half = sin_half * part
    return 1.0 - sin_half * sin_half, sin_half * cos_half


def column_of(row):
    n = row.shape[1]
    eye = lax.broadcasted_iota(jnp.int32, (n, n), 0) == lax.broadcasted_iota(jnp.int32, (n, n), 1)
    return jnp.sum(jnp.where(eye, row, 0.0), axis=1, keepdims=True)


class Fetched:
    def __init__(self, source, target, sem):
        self.copy = pltpu.make_async_copy(source, target, sem)
        self.target = target
        self.waited = False
        self.copy.start()

    def ref(self):
        if not self.waited:
            self.copy.wait()
            self.waited = True
        return self.target

    def __getitem__(self, key):
        return self.ref()[key]


class Sent:
    def __init__(self, source, target, sem):
        self.source, self.target, self.sem = source, target, sem
        self.copies = []

    def __getitem__(self, key):
        return self.source[key]

    def __setitem__(self, key, value):
        self.source[key] = value

    @property
    def shape(self):
        return self.source.shape

    def send(self, *index):
        source, target = self.source, self.target
        if index:
            source, target = source.at[index], target.at[index]
        sem = self.sem.at[len(self.copies)]
        self.copies.append(pltpu.make_async_copy(source, target, sem))
        self.copies[-1].start()


def moving(kernel, first, fetched, n_in, sent, n_out):
    def wrapped(*refs):
        ins, outs, rest = refs[:n_in], refs[n_in : n_in + n_out], refs[n_in + n_out :]
        held = []
        if fetched:
            targets, sems, rest = rest[:fetched], rest[fetched], rest[fetched + 1 :]
            held = [Fetched(ins[first + i], targets[i], sems.at[i]) for i in range(fetched)]
        going = []
        if sent:
            sources, sems, rest = rest[:sent], rest[sent], rest[sent + 1 :]
            going = [Sent(sources[i], outs[i], sems.at[i]) for i in range(sent)]
        kernel(*ins[:first], *held, *ins[first + fetched :], *going, *outs[sent:], *rest)
        for one in held:
            one.ref()
        for one in going:
            for copy in one.copies:
                copy.wait()

    return wrapped


def call(kernel, name, operands, first, fetched, outs, sent, scratch, limit, micros):
    moved = operands[first : first + fetched]
    scratch_shapes = [pltpu.VMEM(a.shape, a.dtype) for a in moved]
    if fetched:
        scratch_shapes.append(pltpu.SemaphoreType.DMA((fetched,)))
    if sent:
        scratch_shapes += [pltpu.VMEM(o.shape, o.dtype) for o in outs[:sent]]
        scratch_shapes.append(pltpu.SemaphoreType.DMA((sent, 6)))
    return pl.pallas_call(
        moving(kernel, first, fetched, len(operands), sent, len(outs)),
        out_shape=tuple(outs),
        in_specs=[SMEM] * first + [HBM] * fetched + [VMEM] * (len(operands) - first - fetched),
        out_specs=tuple([HBM] * sent + [VMEM] * (len(outs) - sent)),
        scratch_shapes=scratch_shapes + scratch,
        cost_estimate=pl.CostEstimate(flops=int(micros * 1.15e9), bytes_accessed=4 << 20, transcendentals=0),
        compiler_params=pltpu.CompilerParams(vmem_limit_bytes=limit),
        name=name,
    )(*operands)


def trace_kernel(fields_ref, send_ref, trace_ref, lower_ref, upper_ref):
    where = lax.broadcasted_iota(jnp.int32, (64, NP), 0) * 32 + lax.broadcasted_iota(
        jnp.int32, (64, NP), 1
    )
    chosen = jnp.zeros((64, NP), f32)
    for face, row in enumerate(face_nodes()):
        for j, node in enumerate(row):
            chosen = jnp.where(where == (face * 16 + j) * 32 + int(node), 1.0, chosen)
    select = chosen.astype(bf16)
    for c in range(6):
        for part, half in enumerate(high_low(fields_ref[c])):
            picked = mm(select, half).astype(bf16)
            for face in range(4):
                trace_ref[part * 96 + c * 16 : part * 96 + (c + 1) * 16, face * ELEMS : (face + 1) * ELEMS] = picked[
                    face * 16 : (face + 1) * 16
                ]
    send = send_ref[...]
    total = [jnp.zeros((192, SHARED), f32), jnp.zeros((192, SHARED), f32)]
    for face in range(4):
        held = trace_ref[:, face * ELEMS : (face + 1) * ELEMS]
        for row in range(2):
            total[row] = total[row] + mm(held, one_hot_rows(ELEMS, face * ELEMS, send[row : row + 1]))
    lower_ref[...] = total[0][:96] + total[0][96:]
    upper_ref[...] = total[1][:96] + total[1][96:]


def lane_faces():
    return lax.shift_right_logical(lax.broadcasted_iota(jnp.int32, (1, 128), 1), 5)


def fold(values):
    row = lax.broadcasted_iota(jnp.int32, (128, 128), 0)
    column = lax.broadcasted_iota(jnp.int32, (128, 128), 1)
    same = jnp.where((row & (HDEV - 1)) == (column & (HDEV - 1)), 1.0, 0.0).astype(bf16)
    high, low = high_low(values)
    return mm(high, same) + mm(low, same)


def project_far(dirs_ref, real, imag):
    theta = [dirs_ref[3 + k : 4 + k, :] for k in range(3)]
    phi = [dirs_ref[6 + k : 7 + k, :] for k in range(2)]

    def onto_theta(v):
        return theta[0] * v[0] + theta[1] * v[1] + theta[2] * v[2]

    def onto_phi(v):
        return phi[0] * v[0] + phi[1] * v[1]

    return (
        onto_theta(real[:3]) + onto_phi(real[3:]),
        onto_theta(imag[:3]) + onto_phi(imag[3:]),
        onto_theta(real[3:]) - onto_phi(real[:3]),
        onto_theta(imag[3:]) - onto_phi(imag[:3]),
    )


def at(values, i):
    return values[i * 8 : (i + 1) * 8]


def own_frequency(rows):
    return (lax.broadcasted_iota(jnp.int32, (rows, 256), 0) & 7) == lax.shift_right_logical(
        lax.broadcasted_iota(jnp.int32, (rows, 256), 1), 5
    )


def fluxes(jump, n, half):
    e = [jump[i * 16 : (i + 1) * 16] for i in range(3)]
    h = [jump[i * 16 : (i + 1) * 16] for i in range(3, 6)]
    normal_e = n[0] * e[0] + n[1] * e[1] + n[2] * e[2]
    normal_h = n[0] * h[0] + n[1] * h[1] + n[2] * h[2]
    flux_e, flux_h = [], []
    for i in range(3):
        a, b = (i + 1) % 3, (i + 2) % 3
        flux_e.append((n[a] * h[b] - n[b] * h[a] + e[i] - normal_e * n[i]) * half)
        flux_h.append((n[b] * e[a] - n[a] * e[b] + h[i] - normal_h * n[i]) * half)
    return flux_e + flux_h


def curls(slope, field_of, metric_of):
    slope_high, slope_low = high_low(slope)
    grads = []
    for c in range(6):
        high, low = high_low(field_of(c))
        grads.append(mm(slope_high, high) + (mm(slope_low, high) + mm(slope_high, low)))

    def along(k, c):
        return (
            metric_of(k) * grads[c][0:32]
            + metric_of(3 + k) * grads[c][32:64]
            + metric_of(6 + k) * grads[c][64:96]
        )

    return [
        along(1, 5) - along(2, 4),
        along(2, 3) - along(0, 5),
        along(0, 4) - along(1, 3),
        along(2, 1) - along(1, 2),
        along(0, 2) - along(2, 0),
        along(1, 0) - along(0, 1),
    ]


def inverse_of(table_ref, m, material):
    base = jnp.zeros(material.shape, f32)
    for k in range(MATS):
        base = jnp.where(material == k, table_ref[m, k], base)
    return base


def halo_operands(below_ref, above_ref):
    below_high, below_low = high_low(below_ref[...])
    above_high, above_low = high_low(above_ref[...])
    return (
        jnp.concatenate([below_high, below_low], axis=0),
        jnp.concatenate([above_high, above_low], axis=0),
    )


def met_at_halo(below, above, mate):
    met = mm(below, one_hot_rows(SHARED, 4 * ELEMS, mate)) + mm(
        above, one_hot_rows(SHARED, 4 * ELEMS + SHARED, mate)
    )
    return met[:96] + met[96:]


def early_kernel(
    wave_ref,
    table_ref,
    fields_ref,
    res_ref,
    partner_ref,
    derivative_ref,
    geometry_ref,
    normals_ref,
    scale_ref,
    interp_ref,
    project_ref,
    lift_ref,
    materials_ref,
    profile_ref,
    slots_ref,
    pos_ref,
    widen_ref,
    widen_q_ref,
    dirs_ref,
    spread_ref,
    spectra_ref,
    trace_ref,
    phase_ref,
    far_ref,
    jump_ref,
    curl_ref,
    weight_ref,
    fields_out,
    res_out,
    rows_ref,
    lift_out_ref,
    project_out_ref,
    slope_ref,
    pad_ref,
    stack_ref,
    group_ref,
):
    heading = dirs_ref[...]
    pos = pos_ref[...]
    path = jnp.zeros((HDEV, DIRS), f32)
    for k in range(3):
        path = path + column_of(pos[k : k + 1]) * heading[k : k + 1]
    for f in range(FREQS):
        cos_part, sin_part = cos_sin_turns(path * (wave_ref[f] * (0.5 / math.pi)))
        rows = slice((f % 8) * HDEV, (f % 8 + 1) * HDEV)
        for place, half in enumerate(high_low(cos_part) + high_low(sin_part)):
            phase_ref[f // 8, place, rows, :] = half

    for i in range(12):
        came = spectra_ref[i]
        for g in range(GROUPS):
            group_ref[g, i * 8 : (i + 1) * 8, :] = came[g * 8 : (g + 1) * 8]
    spread = spread_ref[...].astype(bf16)
    own = own_frequency(192)
    for g in range(GROUPS):
        high, low = high_low(group_ref[g])
        rows = jnp.where(own, mm(jnp.concatenate([high, low], axis=0), spread), 0.0).astype(bf16)
        cos_sum = mm(rows, phase_ref[g, 0])
        cos_sum = cos_sum[:96] + (cos_sum[96:] + mm(rows[:96], phase_ref[g, 1]))
        sin_sum = mm(rows, phase_ref[g, 2])
        sin_sum = sin_sum[:96] + (sin_sum[96:] + mm(rows[:96], phase_ref[g, 3]))
        real = [at(cos_sum, i) - at(sin_sum, i + 6) for i in range(6)]
        imag = [at(sin_sum, i) + at(cos_sum, i + 6) for i in range(6)]
        for c, part in enumerate(project_far(dirs_ref, real, imag)):
            far_ref[c * FREQS + g * 8 : c * FREQS + (g + 1) * 8, :] = part

    lane_face = lane_faces()
    tile = jnp.where(
        (lax.broadcasted_iota(jnp.int32, (HDEV, 128), 1) & (HDEV - 1))
        == lax.broadcasted_iota(jnp.int32, (HDEV, 128), 0),
        1.0,
        0.0,
    )
    slots = mm_exact(jnp.broadcast_to(slots_ref[...].astype(f32), (8, HDEV)), tile)[0:1]
    slots = (slots + 0.5).astype(jnp.int32)
    element = slots & (ELEMS - 1)
    face_id = lax.shift_right_logical(slots, 9)
    pick = one_hot_rows(ELEMS, 0, element)

    def take(values):
        high, low = high_low(values)
        return mm(high, pick) + mm(low, pick)

    stack_ref[...] = jnp.zeros(stack_ref.shape, f32)
    for k in range(3):
        stack_ref[4 * k : 4 * k + 4, :] = normals_ref[k]
    stack_ref[12:16, :] = scale_ref[...]
    stack_ref[16:20, :] = partner_ref[...].astype(f32)
    stack_ref[24:33, :] = geometry_ref[...]
    stack_ref[33:34, :] = materials_ref[...].astype(f32)
    taken = take(stack_ref[...])

    def by_face(first):
        one = lax.broadcasted_iota(jnp.int32, (4, 128), 0) == lane_face
        return jnp.sum(jnp.where(one, taken[first : first + 4], 0.0), axis=0, keepdims=True)

    normal = [by_face(4 * k) for k in range(3)]
    mate_row = by_face(16)
    mate = (mate_row + 0.5).astype(jnp.int32)
    material = (taken[33:34] + 0.5).astype(jnp.int32)
    rows_ref[...] = jnp.zeros(rows_ref.shape, f32)
    for k in range(3):
        rows_ref[k : k + 1, :] = normal[k]
        rows_ref[8 + k : 9 + k, :] = jnp.where(lane_face == face_id, normal[k], 0.0)
    rows_ref[8:16, :] = fold(rows_ref[8:16, :])
    rows_ref[3:4, :] = 0.5 * by_face(12)
    rows_ref[4:5, :] = mate_row
    rows_ref[5:6, :] = face_id.astype(f32)
    for c in range(6):
        fields_out[c] = take(fields_ref[c])
        res_out[c] = take(res_ref[c])
    for m in range(2):
        weight_ref[m] = jnp.zeros((32, 128), f32)
        weight_ref[m, 0:QPTS, :] = take(profile_ref[:, m, :]) * inverse_of(table_ref, m, material)

    interp = interp_ref[...]
    slope_ref[...] = jnp.zeros((96, NP), f32)
    for r in range(3):
        slope_ref[r * 32 : r * 32 + QPTS, :] = mm_exact(interp, derivative_ref[r])
    for c, curl in enumerate(
        curls(slope_ref[...], lambda c: fields_out[c], lambda k: taken[24 + k : 25 + k])
    ):
        curl_ref[c] = curl

    inside = jnp.zeros((192, 128), f32)
    outside = jnp.zeros((192, 128), f32)
    for face in range(4):
        held = trace_ref[:, face * ELEMS : (face + 1) * ELEMS]
        inside = inside + jnp.where(lane_face == face, mm(held, pick), 0.0)
        outside = outside + mm(held, one_hot_rows(ELEMS, face * ELEMS, mate))
    inside = inside[:96] + inside[96:]
    outside = outside[:96] + outside[96:]
    skin = mate == lane_face * ELEMS + element
    jump_ref[:48, :] = jnp.where(skin, -inside[:48], outside[:48]) - inside[:48]
    jump_ref[48:, :] = outside[48:] - inside[48:]

    pad_ref[...] = jnp.zeros((32, NP), f32)
    pad_ref[0:QPTS, :] = interp
    lifted = mm_exact(pad_ref[...], mm_exact(lift_ref[...], widen_ref[...]))
    high, low = high_low(lifted)
    column = lax.broadcasted_iota(jnp.int32, (32, 192), 1)
    lift_out_ref[...] = jnp.where(column < 128, high.astype(f32), low.astype(f32)).astype(bf16)
    projected = mm_exact(project_ref[...], widen_q_ref[...])
    high, low = high_low(projected)
    column = lax.broadcasted_iota(jnp.int32, (NP, 96), 1)
    project_out_ref[...] = jnp.where(column < 64, high.astype(f32), low.astype(f32)).astype(bf16)


def late_kernel(
    below_ref,
    above_ref,
    rows_ref,
    jump_ref,
    curl_ref,
    weight_ref,
    lift_ref,
    project_ref,
    fields_ref,
    res_ref,
    workers_ref,
    phase_time_ref,
    on_face_ref,
    spread_ref,
    dirs_ref,
    spectra_ref,
    phase_ref,
    came_ref,
    spectra_out,
    far_out,
    current_out,
    flux_ref,
    lifted_ref,
    points_ref,
    far_ref,
):
    lane_face = lane_faces()
    below, above = halo_operands(below_ref, above_ref)
    mate = (rows_ref[4:5, :] + 0.5).astype(jnp.int32)
    jump = jump_ref[...] + met_at_halo(below, above, mate)
    normal = [rows_ref[k : k + 1, :] for k in range(3)]
    for c, flux in enumerate(fluxes(jump, normal, rows_ref[3:4, :])):
        lanes = slice(c * 128, (c + 1) * 128)
        for face in range(4):
            high, low = high_low(jnp.where(lane_face == face, flux, 0.0))
            flux_ref[face * 16 : (face + 1) * 16, lanes] = high
            flux_ref[64 + face * 16 : 64 + (face + 1) * 16, lanes] = low
            flux_ref[128 + face * 16 : 128 + (face + 1) * 16, lanes] = high
    lifted = mm(lift_ref[...], flux_ref[...])
    for c in range(6):
        lifted_ref[c * 32 : (c + 1) * 32, :] = lifted[:, c * 128 : (c + 1) * 128]
    lifted_ref[...] = fold(lifted_ref[...])
    for c in range(6):
        lanes = slice(c * 128, (c + 1) * 128)
        values = (curl_ref[c] + lifted_ref[c * 32 : (c + 1) * 32, :]) * weight_ref[c // 3]
        high, low = high_low(values)
        points_ref[0:32, lanes] = high
        points_ref[32:64, lanes] = low
        points_ref[64:96, lanes] = high
    adjusted = mm(project_ref[...], points_ref[...])

    face_id = (rows_ref[5:6, :] + 0.5).astype(jnp.int32)
    on_face = on_face_ref[...]
    mask = jnp.zeros((NP, 128), f32)
    for face in range(4):
        mask = jnp.where(face_id == face, on_face[:NP, face : face + 1], mask)
    mean = []
    for c in range(6):
        new_res = rk_alpha * res_ref[c] + time_step * adjusted[:, c * 128 : (c + 1) * 128]
        new_fields = fields_ref[c] + rk_beta * new_res
        mean.append(jnp.sum(new_fields * mask, axis=0, keepdims=True) * (1.0 / NFP))
    n = [rows_ref[8 + k : 9 + k, :] for k in range(3)]
    current_out[...] = jnp.zeros(current_out.shape, f32)
    current = []
    for sign, field in ((1.0, mean[3:]), (-1.0, mean[:3])):
        for i in range(3):
            a, b = (i + 1) % 3, (i + 2) % 3
            row = ((n[a] * field[b] - n[b] * field[a]) * sign)[:, :HDEV]
            current_out[len(current) : len(current) + 1, :] = row
            current.append(row)

    cos_time, sin_time = cos_sin_turns(phase_time_ref[...] * (0.5 / math.pi))
    turn = (column_of(cos_time), column_of(sin_time))
    for i in range(12):
        spectra_out[i] = spectra_ref[i] + turn[i // 6] * current[i % 6]
    spectra_out.send()

    workers = workers_ref[...].astype(f32)
    same = column_of(workers) == workers
    earlier = lax.broadcasted_iota(jnp.int32, (HDEV, HDEV), 0) < lax.broadcasted_iota(
        jnp.int32, (HDEV, HDEV), 1
    )
    rank = jnp.sum(jnp.where(same & earlier, 1.0, 0.0), axis=0, keepdims=True)
    target = (rank * GRP + workers).astype(jnp.int32)
    placing = one_hot_rows(GRP * CAP, 0, target)
    nt = (((1,), (1,)), ((), ()))
    high, low = high_low(spectra_out[...].reshape(12 * FREQS, HDEV))
    placed = lax.dot_general(placing, high, nt, preferred_element_type=f32) + lax.dot_general(
        placing, low, nt, preferred_element_type=f32
    )
    for j in range(3):
        far_out[pl.ds(CHUNK + j, MEMBERS, stride=ROWS), :] = placed[:, j * 128 : (j + 1) * 128]

    high, low = high_low(current_out[...])
    tiled = mm(jnp.concatenate([high, low], axis=0), spread_ref[...].astype(bf16))
    own = own_frequency(8)
    rows = [jnp.where(own, tiled[i : i + 1], 0.0) for i in range(6)]
    rows += [jnp.where(own, tiled[8 + i : 9 + i], 0.0) for i in range(6)]
    rows = jnp.concatenate(rows, axis=0).astype(bf16)
    for g in range(GROUPS):
        cos_sum = mm(rows, phase_ref[g, 0])
        cos_sum = cos_sum[:48] + (cos_sum[48:] + mm(rows[:48], phase_ref[g, 1]))
        sin_sum = mm(rows, phase_ref[g, 2])
        sin_sum = sin_sum[:48] + (sin_sum[48:] + mm(rows[:48], phase_ref[g, 3]))
        cos_turn, sin_turn = at(turn[0], g), at(turn[1], g)
        real = [cos_turn * at(cos_sum, i) - sin_turn * at(sin_sum, i) for i in range(6)]
        imag = [cos_turn * at(sin_sum, i) + sin_turn * at(cos_sum, i) for i in range(6)]
        for c, part in enumerate(project_far(dirs_ref, real, imag)):
            rows_of = slice(c * FREQS + g * 8, c * FREQS + (g + 1) * 8)
            far_ref[rows_of, :] = came_ref[rows_of, :] + part
    far = far_ref[...].T
    for r in range(CHUNK):
        far_out[pl.ds(r, MEMBERS, stride=ROWS), :] = far[r * MEMBERS : (r + 1) * MEMBERS]


def bulk_kernel(
    table_ref,
    current_ref,
    below_ref,
    above_ref,
    fields_ref,
    res_ref,
    partner_ref,
    geometry_ref,
    normals_ref,
    scale_ref,
    materials_ref,
    profile_ref,
    trace_ref,
    lift_ref,
    project_ref,
    slope_ref,
    fields_out,
    res_out,
    mark_ref,
    flux_ref,
    points_ref,
    weight_ref,
):
    mark_ref[...] = current_ref[...]
    flux_ref[...] = jnp.zeros(flux_ref.shape, bf16)
    below, above = halo_operands(below_ref, above_ref)
    for face in range(4):
        lanes = slice(face * ELEMS, (face + 1) * ELEMS)
        mate = partner_ref[face : face + 1, :]
        total = jnp.zeros((192, ELEMS), f32)
        for source in range(4):
            held = trace_ref[:, source * ELEMS : (source + 1) * ELEMS]
            total = total + mm(held, one_hot_rows(ELEMS, source * ELEMS, mate))
        outside = total[:96] + total[96:] + met_at_halo(below, above, mate)
        own = trace_ref[:, lanes].astype(f32)
        inside = own[:96] + own[96:]
        skin = mate == lax.broadcasted_iota(jnp.int32, (1, ELEMS), 1) + face * ELEMS
        jump = jnp.concatenate(
            [jnp.where(skin, -inside[:48], outside[:48]) - inside[:48], outside[48:] - inside[48:]], axis=0
        )
        normal = [normals_ref[k, face : face + 1, :] for k in range(3)]
        half = 0.5 * scale_ref[face : face + 1, :]
        for c, flux in enumerate(fluxes(jump, normal, half)):
            high, low = high_low(flux)
            flux_ref[c, face * 16 : (face + 1) * 16, :] = high
            flux_ref[c, 64 + face * 16 : 64 + (face + 1) * 16, :] = low
            flux_ref[c, 128 + face * 16 : 128 + (face + 1) * 16, :] = high
    material = materials_ref[...]
    for m in range(2):
        weight_ref[m] = jnp.zeros((32, ELEMS), f32)
        weight_ref[m, 0:QPTS, :] = profile_ref[:, m, :] * inverse_of(table_ref, m, material)
    curl = curls(slope_ref[...], lambda c: fields_ref[c], lambda k: geometry_ref[k : k + 1, :])
    lift = lift_ref[...]
    project = project_ref[...]
    for c in range(6):
        values = (curl[c] + mm(lift, flux_ref[c])) * weight_ref[c // 3]
        high, low = high_low(values)
        points_ref[c, 0:32, :] = high
        points_ref[c, 32:64, :] = low
        points_ref[c, 64:96, :] = high
        new_res = rk_alpha * res_ref[c] + time_step * mm(project, points_ref[c])
        res_out[c] = new_res
        res_out.send(c)
        fields_out[c] = fields_ref[c] + rk_beta * new_res
        fields_out.send(c)


def sum_kernel(arrived_ref, mark_ref, sum_ref, pieces_ref):
    rows = [
        jnp.sum(arrived_ref[pl.ds(r, MEMBERS, stride=ROWS), :], axis=0, keepdims=True) for r in range(CHUNK)
    ]
    total = jnp.concatenate(rows, axis=0)
    for z in range(sum_ref.shape[0]):
        sum_ref[z] = total
    for j in range(3):
        piece = arrived_ref[pl.ds(CHUNK + j, MEMBERS, stride=ROWS), :]
        pieces_ref[:, j] = piece.reshape(MEMBERS // GRP, GRP, 128)


def core_first(chunk):
    return chunk % 2 * (MEMBERS // GRP // 2) + chunk // 2


def join_kernel(arrived_ref, pieces_ref, message_ref):
    total = jnp.sum(arrived_ref[...], axis=0)
    for p in range(message_ref.shape[0]):
        message_ref[core_first(p), 0] = total
        message_ref[core_first(p), 1:] = pieces_ref[p]


def final_kernel(arrived_ref, far_ref, worker_ref, rows_ref):
    for p in range(arrived_ref.shape[0]):
        far_ref[p * CHUNK : (p + 1) * CHUNK, :] = arrived_ref[core_first(p), 0]
        for j in range(3):
            rows_ref[j, pl.ds(p, GRP, stride=CAP), :] = arrived_ref[core_first(p), 1 + j]
    for j in range(3):
        worker_ref[4 * j : 4 * j + 4] = rows_ref[j].T.reshape(4, FREQS, GRP * CAP)


def sds(shape, dtype=f32):
    return jax.ShapeDtypeStruct(shape, dtype)


VMEM = pl.BlockSpec(memory_space=pltpu.VMEM)
SMEM = pl.BlockSpec(memory_space=pltpu.SMEM)
HBM = pl.BlockSpec(memory_space=pltpu.HBM)
WHOLE = 67043328
PART = 36 << 20


def factors(dom):
    return (dom // 8, 4, 2)


def per_device(
    fields,
    section_res,
    derivative,
    geometry,
    normals,
    face_scale,
    lift_matrix,
    interp_q,
    project_q,
    mat_table,
    materials,
    profile,
    face_partner,
    send_faces,
    spectra,
    huy_slots,
    huy_worker,
    huy_pos,
    wavenumber,
    time_phase,
    sizes,
):
    along_z, along_x, cores = sizes
    partitions = along_z * along_x * cores * GRP
    order = np.arange(DIRS).reshape(GRP, MEMBERS // GRP, CHUNK).transpose(2, 1, 0).reshape(-1)
    on_face, widen, widen_q, spread, directions = constants(
        order, 1.0 / math.sqrt(HDEV * partitions)
    )
    slots_row = huy_slots.reshape(1, HDEV)

    traces, lower, upper = call(
        trace_kernel,
        "traces",
        (fields, send_faces),
        0,
        0,
        (sds((192, 4 * ELEMS), bf16), sds((96, SHARED)), sds((96, SHARED))),
        0,
        [],
        PART,
        2,
    )

    ring = ("z", "x", "core", "y")
    from_below = lax.ppermute(upper, ring, [(i, i + 1) for i in range(partitions - 1)])
    from_above = lax.ppermute(lower, ring, [(i + 1, i) for i in range(partitions - 1)])

    partner = face_partner
    material_row = materials.reshape(1, ELEMS)
    coating = profile.transpose(1, 0, 2)
    came = spectra.transpose(1, 0, 2)
    phases, far_came, jump, curl, weight, fields_at, res_at, rows, lift3, project3, slope = call(
        early_kernel,
        "early",
        (
            wavenumber,
            mat_table,
            fields,
            section_res,
            partner,
            derivative,
            geometry,
            normals,
            face_scale,
            interp_q,
            project_q,
            lift_matrix,
            material_row,
            coating,
            slots_row,
            huy_pos,
            widen,
            widen_q,
            directions,
            spread,
            came,
            traces,
        ),
        2,
        0,
        (
            sds((GROUPS, 4, 8 * HDEV, DIRS), bf16),
            sds((4 * FREQS, DIRS)),
            sds((96, 128)),
            sds((6, 32, 128)),
            sds((2, 32, 128)),
            sds((6, NP, 128)),
            sds((6, NP, 128)),
            sds((16, 128)),
            sds((32, 192), bf16),
            sds((NP, 96), bf16),
            sds((96, NP)),
        ),
        0,
        [pltpu.VMEM((32, NP), f32), pltpu.VMEM((40, ELEMS), f32), pltpu.VMEM((GROUPS, 96, HDEV), f32)],
        PART,
        6,
    )

    spectra_t, message, current = call(
        late_kernel,
        "late",
        (
            from_below,
            from_above,
            rows,
            jump,
            curl,
            weight,
            lift3,
            project3,
            fields_at,
            res_at,
            huy_worker.reshape(1, HDEV),
            time_phase.reshape(1, FREQS),
            on_face,
            spread,
            directions,
            came,
            phases,
            far_came,
        ),
        0,
        0,
        (sds((12, FREQS, HDEV)), sds((MEMBERS * ROWS, 4 * FREQS)), sds((8, HDEV))),
        1,
        [
            pltpu.VMEM((192, 768), bf16),
            pltpu.VMEM((192, 128), f32),
            pltpu.VMEM((96, 768), bf16),
            pltpu.VMEM((4 * FREQS, DIRS), f32),
        ],
        PART,
        3,
    )

    new_fields, new_res, mark = call(
        bulk_kernel,
        "bulk",
        (
            mat_table,
            current,
            from_below,
            from_above,
            fields,
            section_res,
            partner,
            geometry,
            normals,
            face_scale,
            material_row,
            coating,
            traces,
            lift3,
            project3,
            slope,
        ),
        1,
        0,
        (sds((6, NP, ELEMS)), sds((6, NP, ELEMS)), sds((8, HDEV))),
        2,
        [
            pltpu.VMEM((6, 192, ELEMS), bf16),
            pltpu.VMEM((6, 96, ELEMS), bf16),
            pltpu.VMEM((2, 32, ELEMS), f32),
        ],
        PART,
        6,
    )
    new_spectra = spectra_t.transpose(1, 0, 2)

    chunks = MEMBERS // GRP
    small = dict(compiler_params=pltpu.CompilerParams(vmem_limit_bytes=8 << 20))
    arrived = lax.all_to_all(
        message.reshape(MEMBERS, 1, ROWS * 128), ("x", "core", "y"), 0, 0, tiled=True
    ).reshape(MEMBERS * ROWS, 128)
    part, pieces = pl.pallas_call(
        sum_kernel,
        out_shape=(sds((along_z, CHUNK, 128)), sds((chunks, 3, GRP, 128))),
        in_specs=[VMEM, VMEM],
        out_specs=(VMEM, VMEM),
        name="sum",
        **small,
    )(arrived, mark)
    part = lax.all_to_all(part, "z", 0, 0, tiled=True)
    message = pl.pallas_call(
        join_kernel,
        out_shape=sds((chunks, 4, CHUNK, 128)),
        in_specs=[VMEM, VMEM],
        out_specs=VMEM,
        name="join",
        **small,
    )(part, pieces)
    arrived = lax.all_to_all(message, ("core", "x"), 0, 0, tiled=True)
    far_field, worker_t = pl.pallas_call(
        final_kernel,
        out_shape=(sds((chunks * CHUNK, 128)), sds((12, FREQS, GRP * CAP))),
        in_specs=[VMEM],
        out_specs=(VMEM, VMEM),
        scratch_shapes=[pltpu.VMEM((3, GRP * CAP, 128), f32)],
        name="final",
        **small,
    )(arrived)
    worker_spectra = worker_t.transpose(1, 0, 2)
    return (new_fields, new_res, new_spectra, worker_spectra, far_field)


def solution(mesh):
    dom = mesh.shape["dom"]
    sizes = factors(dom)
    fine = Mesh(mesh.devices.reshape(*sizes, GRP), ("z", "x", "core", "y"))
    every = ("z", "x", "core", "y")
    last = {1: P(every), 2: P(None, every), 3: P(None, None, every)}
    return jax.shard_map(
        lambda *args: per_device(*args, sizes=sizes),
        mesh=fine,
        in_specs=(
            last[3],
            last[3],
            P(),
            last[2],
            last[3],
            last[2],
            P(),
            P(),
            P(),
            P(),
            last[1],
            last[3],
            last[2],
            last[2],
            last[3],
            last[1],
            P(every, None),
            last[2],
            P(),
            P(),
        ),
        out_specs=(last[3], last[3], last[3], last[3], P("y", None)),
        check_vma=False,
    )
```
